32 devices in a mesh: rep: 4 (over x, core), own: 8 (over z, y).
Axes of the slice: x: 2, y: 2, z: 4, core: 2. Of those that a mesh axis runs over, the one named last changes fastest.
Arguments:
- replica_delta: float32 [4, 8, 64, 1792], P('rep', None, 'own'), may hold values from -6 to 6
- layer_basis: float32 [4, 1792, 64], replicated, may hold values from -0.25 to 0.25
- layer_of: int32 [8], replicated, may hold values from 0 to 3
- owner_of: int32 [8], replicated, may hold values from 0 to 7, as said below
- weights_owned: float32 [16, 64, 1792], P('own'), may hold values from -6 to 6
- momentum_owned: float32 [16, 64, 1792], P('own'), may hold values from -4 to 4
Outputs:
- new_weights: float32 [16, 64, 1792], P('own')
- new_momentum: float32 [16, 64, 1792], P('own')
- replica_weights: float32 [8, 64, 1792], P(None, 'own')
The draws below stay inside these ranges and needn't reach their ends.
Inputs may be any that keep to these rules, and one draw needn't show every extreme that they name: `owner_of`: no owner holds more than 2 blocks, and some owner holds exactly 2; the slots of an owner are taken in the order of the blocks.
All inputs are finite; a program needn't handle non-finite values.
Results may differ from the reference program's by a relative error of at most 0.00007.
Values sent between devices are 32-bit elements; how exact they have to be, the bound alone decides.
No kernel may reach another device: no remote copies, remote signals or barrier semaphores. Data moves between devices by JAX's collectives and lax.ppermute only.
A program may use at most 128 MiB of HBM per device.

```python
import jax
import jax.numpy as jnp
from jax import lax

D = 1792
RANK = 64
LAYERS = 4
CAP = 2
ROWS = 64
BLOCKS = 8
SLOTS = 16
N_REP = 4
N_OWN = 8


def draw_owner_of(key, part):
    first_key, order_key, shuffle_key = jax.random.split(key, 3)
    slot_total = N_OWN * CAP
    favoured = jax.random.randint(first_key, (), 0, N_OWN)
    slot_order = jax.random.permutation(order_key, slot_total)
    position = jnp.zeros((slot_total,), jnp.int32).at[slot_order].set(jnp.arange(slot_total, dtype=jnp.int32))
    slot_index = jnp.arange(slot_total, dtype=jnp.int32)
    slot_score = jnp.where(slot_index // CAP == favoured, slot_index % CAP - CAP, position)
    picked = jnp.argsort(slot_score, stable=True)[:BLOCKS]
    owners = (picked // CAP).astype(jnp.int32)
    return owners[jax.random.permutation(shuffle_key, BLOCKS)]


def with_ends(array, rng, low, high):
    place = [jax.random.randint(jax.random.fold_in(rng, axis), (), 0, length) for axis, length in enumerate(array.shape)]
    main_axis = array.shape.index(max(array.shape))
    next_to = place[:main_axis] + [(place[main_axis] + 1) % array.shape[main_axis]] + place[main_axis + 1:]
    return array.at[tuple(place)].set(low).at[tuple(next_to)].set(high)


def steps_of(rng, extent, cuts, least, largest):
    level = 1.0
    for dim, parts in cuts:
        draws = jax.random.uniform(jax.random.fold_in(jax.random.fold_in(rng, 6), dim), (parts,), jnp.float32, least / len(cuts), largest / len(cuts))
        level = level * jnp.repeat(jnp.exp(draws), extent[dim] // parts).reshape((-1,) + (1,) * (len(extent) - 1 - dim))
    return level


def gaussian(rng, shape, scale, bound, shards=(), kind=jnp.bfloat16):
    values = jax.random.normal(rng, shape, jnp.float32) * scale
    if len(shards) > 0:
        values = steps_of(rng, shape, shards, -0.22, 0.18) * values
    return jnp.clip(values, min=-bound, max=bound).astype(kind)


def setup_inputs(seed: int = 0) -> dict:
    keys = jax.random.split(jax.random.key(seed), 7)
    replica_delta = gaussian(keys[0], (N_REP, BLOCKS, ROWS, D), 1.0, 6.0, ((0, 4), (2, 8)), jnp.float32)
    layer_basis = gaussian(keys[1], (LAYERS, D, RANK), (8 * RANK) ** -0.5, 0.25, (), jnp.float32)
    layer_of = with_ends(jax.random.randint(keys[2], (BLOCKS,), 0, LAYERS), jax.random.fold_in(keys[2], 1), 0, LAYERS - 1).astype(jnp.int32)
    owner_of = draw_owner_of(jax.random.fold_in(keys[6], 71), 0)
    weights_owned = gaussian(keys[4], (SLOTS, ROWS, D), 1.0, 6.0, ((0, 8),), jnp.float32)
    momentum_owned = gaussian(keys[5], (SLOTS, ROWS, D), 0.3, 4.0, ((0, 8),), jnp.float32)
    return dict(replica_delta=replica_delta, layer_basis=layer_basis, layer_of=layer_of, owner_of=owner_of, weights_owned=weights_owned, momentum_owned=momentum_owned)


momentum_decay = 0.9
outer_rate = 0.7


def reference(replica_delta, layer_basis, layer_of, owner_of, weights_owned, momentum_owned):
    highest = lax.Precision.HIGHEST
    blocks = owner_of.shape[0]
    same_owner = owner_of[None, :] == owner_of[:, None]
    positions = jnp.arange(blocks, dtype=jnp.int32)
    earlier = positions[None, :] < positions[:, None]
    rank_in = jnp.sum((same_owner & earlier).astype(jnp.int32), axis=1).astype(jnp.int32)
    slot_of = (owner_of * CAP + rank_in).astype(jnp.int32)
    chosen = layer_basis[layer_of.astype(jnp.int32)]
    coeffs = jnp.einsum("rbnd,bdk->rbnk", replica_delta, chosen, precision=highest)
    averaged = jnp.sum(coeffs, axis=0) / N_REP
    outer_grad = jnp.einsum("bnk,bdk->bnd", averaged, chosen, precision=highest)
    slot_total = weights_owned.shape[0]
    holding = (slot_of[None, :] == jnp.arange(slot_total, dtype=jnp.int32)[:, None]).astype(jnp.float32)
    outer_slot = jnp.einsum("sb,bnd->snd", holding, outer_grad, precision=highest)
    in_use = jnp.sum(holding, axis=1)[:, None, None]
    new_momentum = (momentum_decay * momentum_owned + outer_slot) * in_use
    new_weights = (weights_owned - outer_rate * (outer_slot + momentum_decay * new_momentum)) * in_use
    replica_weights = new_weights[slot_of]
    return new_weights, new_momentum, replica_weights
```

```python
import math

import jax
import jax.numpy as jnp
from jax import lax
from jax.experimental import pallas as pl
from jax.experimental.pallas import tpu as pltpu
from jax.sharding import PartitionSpec as P

momentum_decay = 0.9
outer_rate = 0.7
carried = outer_rate * momentum_decay * momentum_decay
total_rate = outer_rate * (1.0 + momentum_decay)

HIGHEST = lax.Precision.HIGHEST
VMEM = pl.BlockSpec(memory_space=pltpu.VMEM)
SMEM = pl.BlockSpec(memory_space=pltpu.SMEM)


def params(*arrays):
    held = sum(4 * math.prod(array.shape) for array in arrays)
    return pltpu.CompilerParams(vmem_limit_bytes=2 * held + 4 * 1024 * 1024)


def half_index():
    return lax.rem(lax.axis_index("rep"), 2)


def place_of(owner_ref, block):
    owner = owner_ref[block]
    slot = jnp.int32(0)
    for earlier in range(block):
        slot = slot + jnp.where(owner_ref[earlier] == owner, 1, 0)
    return owner, slot


def mixed_kernel(rows, weights_ref, momentum_ref, mixed_ref):
    columns = mixed_ref.shape[-1]
    for half in range(2):

        @pl.when(half_index() == half)
        def _():
            part = pl.ds(half * columns, columns)
            for target in range(mixed_ref.shape[0]):
                here = pl.ds(target * rows, rows)
                mixed_ref[target] = (
                    weights_ref[:, here, part] - carried * momentum_ref[:, here, part]
                )


def project_kernel(owner_ref, layer_ref, delta_ref, basis_ref, coeffs_ref):
    blocks, rows, width = delta_ref.shape
    layers, rank, _ = basis_ref.shape
    products = lax.dot_general(
        delta_ref[...].reshape(blocks * rows, width),
        basis_ref[...].reshape(layers * rank, width),
        (((1,), (1,)), ((), ())),
        precision=HIGHEST,
        preferred_element_type=jnp.float32,
    )
    lane = lax.broadcasted_iota(jnp.int32, (rows, layers * rank), 1)
    coeffs_ref[...] = jnp.zeros_like(coeffs_ref)
    for block in range(blocks):
        owner, slot = place_of(owner_ref, block)
        own = products[block * rows:(block + 1) * rows]
        own = jnp.where(lane // rank == layer_ref[block], own, 0.0)
        folded = own[:, :2 * rank]
        for pair in range(1, layers // 2):
            folded = folded + own[:, 2 * rank * pair:2 * rank * (pair + 1)]
        folded = folded + pltpu.roll(folded, rank, 1)
        placed = jnp.where(lane[:, :2 * rank] // rank == slot, folded, 0.0)
        coeffs_ref[owner] = coeffs_ref[owner] + placed


def spread(pair, slot, layer, layers, rank):
    lane = lax.broadcasted_iota(jnp.int32, pair.shape, 1)
    both = jnp.where(lane // rank == slot, pair, 0.0)
    both = both + pltpu.roll(both, rank, 1)
    wide = jnp.concatenate([both] * (layers // 2), axis=1)
    lane = lax.broadcasted_iota(jnp.int32, wide.shape, 1)
    return jnp.where(lane // rank == layer, wide, 0.0)


def owner_kernel(
    reps, owner_ref, layer_ref, pieces_ref, basis_ref, weights_ref, momentum_ref,
    new_weights_ref, new_momentum_ref, whole_ref,
):
    layers, rank, width = basis_ref.shape
    slots, rows, _ = weights_ref.shape
    far, _, piece_rows, _ = pieces_ref.shape
    me = lax.axis_index("own")
    for step in range(far):
        for side in range(2):
            source = me ^ (2 * step + side)
            whole_ref[pl.ds(source * piece_rows, piece_rows), :] = pieces_ref[step, side]
    basis = basis_ref[...].reshape(layers * rank, width)
    averaged = whole_ref[...] * (1.0 / reps)
    for slot in range(slots):
        used = jnp.int32(0)
        layer = jnp.int32(-1)
        for block in range(owner_ref.shape[0]):
            owner, place = place_of(owner_ref, block)
            here = (owner == me) & (place == slot)
            layer = jnp.where(here, layer_ref[block], layer)
            used = jnp.where(here, 1, used)
        grad = jnp.dot(
            spread(averaged, slot, layer, layers, rank), basis,
            precision=HIGHEST, preferred_element_type=jnp.float32,
        )
        momentum = momentum_decay * momentum_ref[slot] + grad
        weights = weights_ref[slot] - outer_rate * (grad + momentum_decay * momentum)
        new_momentum_ref[slot] = jnp.where(used == 1, momentum, 0.0)
        new_weights_ref[slot] = jnp.where(used == 1, weights, 0.0)


def rows_kernel(
    reps, owner_ref, layer_ref, coeffs_ref, basis_ref, near_ref, other_ref,
    replica_ref, wide_ref, grad_ref,
):
    layers, rank, width = basis_ref.shape
    blocks, rows, _ = replica_ref.shape
    columns = near_ref.shape[-1]
    for block in range(blocks):
        owner, slot = place_of(owner_ref, block)
        wide_ref[pl.ds(block * rows, rows), :] = spread(
            coeffs_ref[owner], slot, layer_ref[block], layers, rank
        )
    basis = basis_ref[...].reshape(layers * rank, width)
    grad_ref[...] = jnp.dot(
        wide_ref[...] * (total_rate / reps), basis,
        precision=HIGHEST, preferred_element_type=jnp.float32,
    )
    for half in range(2):

        @pl.when(half_index() == half)
        def _():
            for block in range(blocks):
                owner, slot = place_of(owner_ref, block)
                for part, mixed_ref in ((half, near_ref), (1 - half, other_ref)):
                    here = pl.ds(part * columns, columns)
                    replica_ref[block, :, here] = (
                        mixed_ref[owner, slot] - grad_ref[pl.ds(block * rows, rows), here]
                    )


def local(replica_delta, layer_basis, layer_of, owner_of, weights_owned, momentum_owned):
    own_count = lax.axis_size("own")
    rep_count = lax.axis_size("rep")
    far = own_count // 2
    slots, owned_rows, width = weights_owned.shape
    blocks, rows = replica_delta.shape[1:3]
    layers, _, rank = layer_basis.shape
    f32 = jnp.float32
    basis = jnp.swapaxes(layer_basis, 1, 2)
    me = lax.axis_index("own")
    side, depth = lax.rem(me, 2), me // 2

    def swap(array, axes, rep_bits, own_bits):
        pairs = []
        for rep in range(rep_count):
            for own in range(own_count):
                source = rep * own_count + own
                pairs.append((source, (rep ^ rep_bits) * own_count + (own ^ own_bits)))
        return lax.ppermute(array, axes, pairs)

    both = ("rep", "own")
    mixed = pl.pallas_call(
        lambda *refs: mixed_kernel(rows, *refs),
        out_shape=jax.ShapeDtypeStruct((own_count, slots, rows, width // 2), f32),
        in_specs=[VMEM, VMEM],
        out_specs=VMEM,
        compiler_params=params(weights_owned, momentum_owned, weights_owned),
        name="mixed",
    )(weights_owned, momentum_owned)
    near = lax.all_to_all(mixed, "own", split_axis=0, concat_axis=0, tiled=True)
    other = swap(near, both, 1, 0)

    coeffs = pl.pallas_call(
        project_kernel,
        out_shape=jax.ShapeDtypeStruct((own_count, rows, slots * rank), f32),
        in_specs=[SMEM, SMEM, VMEM, VMEM],
        out_specs=VMEM,
        compiler_params=params(replica_delta, basis),
        name="project",
    )(owner_of, layer_of, replica_delta[0], basis)
    coeffs = coeffs + swap(coeffs, both, 1, 0)
    halves = coeffs.reshape(far, 2, rows, slots * rank)
    beside = lax.dynamic_index_in_dim(halves, 1 - side, 1, keepdims=False)
    across = swap(coeffs, both, 2, 0)
    arrived = swap(beside, both, 0, 1), swap(beside, both, 2, 1)
    coeffs = coeffs + across
    halves = coeffs.reshape(far, 2, rows, slots * rank)
    mine = lax.dynamic_index_in_dim(halves, side, 1, keepdims=False)
    pieces = jnp.stack([mine, arrived[0] + arrived[1]], axis=1)
    gathered = [lax.dynamic_index_in_dim(pieces, depth, 0, keepdims=False)]
    for step in range(1, far):
        sent = lax.dynamic_index_in_dim(pieces, depth ^ step, 0, keepdims=False)
        gathered.append(swap(sent, both, 0, 2 * step))
    gathered = jnp.stack(gathered)

    new_weights, new_momentum = pl.pallas_call(
        lambda *refs: owner_kernel(rep_count, *refs),
        out_shape=[jax.ShapeDtypeStruct(weights_owned.shape, f32)] * 2,
        in_specs=[SMEM, SMEM, VMEM, VMEM, VMEM, VMEM],
        out_specs=[VMEM, VMEM],
        scratch_shapes=[pltpu.VMEM((owned_rows, slots * rank), f32)],
        compiler_params=params(basis, *[weights_owned] * 4),
        name="owner",
    )(owner_of, layer_of, gathered, basis, weights_owned, momentum_owned)
    replica_weights = pl.pallas_call(
        lambda *refs: rows_kernel(rep_count, *refs),
        out_shape=jax.ShapeDtypeStruct((blocks, rows, width), f32),
        in_specs=[SMEM, SMEM, VMEM, VMEM, VMEM, VMEM],
        out_specs=VMEM,
        scratch_shapes=[
            pltpu.VMEM((blocks * rows, layers * rank), f32),
            pltpu.VMEM((blocks * rows, width), f32),
        ],
        compiler_params=params(basis, near, other, replica_delta),
        name="rows",
    )(owner_of, layer_of, coeffs, basis, near, other)
    return (new_weights, new_momentum, replica_weights)


def solution(mesh):
    placed = (
        P("rep", None, "own", None),
        P(),
        P(),
        P(),
        P("own", None, None),
        P("own", None, None),
    )
    return jax.shard_map(
        local,
        mesh=mesh,
        in_specs=placed,
        out_specs=(P("own", None, None), P("own", None, None), P(None, "own", None)),
        check_vma=False,
    )
```

```python
import math

import jax
import jax.numpy as jnp
from jax import lax
from jax.experimental import pallas as pl
from jax.experimental.pallas import tpu as pltpu
from jax.sharding import PartitionSpec as P

momentum_decay = 0.9
outer_rate = 0.7
carried = outer_rate * momentum_decay * momentum_decay
total_rate = outer_rate * (1.0 + momentum_decay)

VMEM = pl.BlockSpec(memory_space=pltpu.VMEM)
SMEM = pl.BlockSpec(memory_space=pltpu.SMEM)
HBM = pl.BlockSpec(memory_space=pltpu.HBM)
ANY = pl.BlockSpec(memory_space=pl.ANY)


def params(*arrays):
    held = sum(4 * math.prod(array.shape) for array in arrays)
    return pltpu.CompilerParams(vmem_limit_bytes=2 * held + 4 * 1024 * 1024)


def position():
    rep = lax.axis_index("rep")
    return lax.rem(rep, 2), rep // 2


def split(array):
    high = array.astype(jnp.bfloat16)
    low = (array - high.astype(jnp.float32)).astype(jnp.bfloat16)
    return high, low


def product(left, right_high, right_low, contract):
    rows = left.shape[0]
    high, low = split(left)

    def dot(a, b):
        return lax.dot_general(
            a, b, (contract, ((), ())), preferred_element_type=jnp.float32
        )

    both = dot(jnp.concatenate([high, low], axis=0), right_high)
    return both[:rows] + (both[rows:] + dot(high, right_low))


def place_of(owner_ref, block):
    owner = owner_ref[block]
    slot = jnp.int32(0)
    for earlier in range(block):
        slot = slot + jnp.where(owner_ref[earlier] == owner, 1, 0)
    return owner, slot


def outset_kernel(
    owner_ref, layer_ref, delta_ref, basis_ref, weights_ref, momentum_ref,
    sent_ref, coeffs_ref,
    owner_smem, layer_smem, delta_vmem, basis_vmem, w_ref, m_ref, made_ref, in_sems, out_sems,
):
    across_count, owners, rows, total = sent_ref.shape
    blocks, _, width = delta_ref.shape
    layers, rank, _ = basis_ref.shape
    columns = width // 2
    core, across = position()
    part = pl.ds(pl.multiple_of(core * columns, 128), columns)
    loads = [
        pltpu.make_async_copy(source, target, in_sems.at[index])
        for index, (source, target) in enumerate((
            (weights_ref.at[across, :, part], w_ref),
            (momentum_ref.at[across, :, part], m_ref),
            (owner_ref, owner_smem),
            (layer_ref, layer_smem),
            (delta_ref, delta_vmem),
            *[(basis_ref.at[layer], basis_vmem.at[layer]) for layer in range(layers)],
        ))
    ]
    for load in loads:
        load.start()
    loads[0].wait()
    loads[1].wait()
    for owner in range(owners):
        here = pl.ds(owner * rows, rows)
        made_ref[owner, :, :columns] = w_ref[here, :] - carried * m_ref[here, :]
    for load in loads[2:]:
        load.wait()
    high, low = split(basis_vmem[...].reshape(layers * rank, width))
    products = product(
        delta_vmem[...].reshape(blocks * rows, width), high, low, ((1,), (1,))
    )
    lane = lax.broadcasted_iota(jnp.int32, (rows, layers * rank), 1)
    coeffs_ref[...] = jnp.zeros_like(coeffs_ref)
    for block in range(blocks):
        owner, slot = place_of(owner_smem, block)
        own = products[block * rows:(block + 1) * rows]
        own = jnp.where(lane // rank == layer_smem[block], own, 0.0)
        folded = own[:, :2 * rank]
        for pair in range(1, layers // 2):
            folded = folded + own[:, 2 * rank * pair:2 * rank * (pair + 1)]
        folded = folded + pltpu.roll(folded, rank, 1)
        placed = jnp.where(lane[:, :2 * rank] // rank == slot, folded, 0.0)
        coeffs_ref[owner] = coeffs_ref[owner] + placed
    made_ref[:, :, columns:] = coeffs_ref[...]
    stores = []
    for target in range(across_count):
        store = pltpu.make_async_copy(made_ref, sent_ref.at[target], out_sems.at[target])
        store.start()
        stores.append(store)
    for store in stores:
        store.wait()


def held_by(me, slot, owner_ref, layer_ref):
    used, layer = jnp.int32(0), jnp.int32(0)
    for block in range(owner_ref.shape[0]):
        owner, place = place_of(owner_ref, block)
        here = (owner == me) & (place == slot)
        layer = jnp.where(here, layer_ref[block], layer)
        used = jnp.where(here, 1, used)
    return used, layer


def prepare_kernel(
    reps, owner_ref, layer_ref, coeffs_ref, basis_ref, momentum_ref,
    grad_ref, high_ref, low_ref, held_ref, wide_ref, basis_vmem, sems, basis_sem,
):
    blocks, rows, width = grad_ref.shape
    layers, rank, _ = basis_ref.shape
    me = lax.axis_index("own")
    loads = []
    for slot in range(momentum_ref.shape[0]):
        load = pltpu.make_async_copy(momentum_ref.at[slot], held_ref.at[slot], sems.at[slot])
        load.start()
        loads.append(load)
    basis_load = pltpu.make_async_copy(basis_ref, basis_vmem, basis_sem)
    basis_load.start()
    lane = lax.broadcasted_iota(jnp.int32, (rows, 2 * rank), 1)
    wide_lane = lax.broadcasted_iota(jnp.int32, (rows, layers * rank), 1)
    for block in range(blocks):
        owner, slot = place_of(owner_ref, block)
        both = jnp.where(lane // rank == slot, coeffs_ref[owner], 0.0)
        both = both + pltpu.roll(both, rank, 1)
        wide = jnp.concatenate([both] * (layers // 2), axis=1)
        wide_ref[pl.ds(block * rows, rows), :] = jnp.where(
            wide_lane // rank == layer_ref[block], wide, 0.0
        )
    basis_load.wait()
    high, low = split(basis_vmem[...].reshape(layers * rank, width))
    grad = product(wide_ref[...] * (total_rate / reps), high, low, ((1,), (0,)))
    grad_ref[...] = grad.reshape(blocks, rows, width)
    for slot in range(momentum_ref.shape[0]):
        _, layer = held_by(me, slot, owner_ref, layer_ref)
        slot_high, slot_low = split(basis_vmem[layer])
        high_ref[slot] = slot_high
        low_ref[slot] = slot_low
    for load in loads:
        load.wait()


def after_kernel(near_ref, grad_ref, same_ref):
    pass


def final_kernel(
    reps, owner_ref, layer_ref, near_ref, far_ref, high_ref, low_ref, momentum_ref, grad_ref,
    weights_ref, new_weights_ref, new_momentum_ref, replica_ref,
    owner_smem, layer_smem, w_ref, m_ref, rows_ref, in_sems, out_sems, rows_sem,
):
    slots, rows, width = weights_ref.shape
    rank = high_ref.shape[1]
    blocks = replica_ref.shape[0]
    columns = width // 2
    me = lax.axis_index("own")
    core, _ = position()
    sources = [(owner_ref, owner_smem), (layer_ref, layer_smem)]
    sources += [(weights_ref.at[slot], w_ref.at[slot]) for slot in range(slots)]
    loads = [
        pltpu.make_async_copy(source, target, in_sems.at[index])
        for index, (source, target) in enumerate(sources)
    ]
    for load in loads:
        load.start()
    summed = (near_ref[0, :, :, columns:] + near_ref[1, :, :, columns:]) + (
        far_ref[0, :, :, columns:] + far_ref[1, :, :, columns:]
    )
    averaged = summed.reshape(rows, slots * rank) * (1.0 / reps)
    loads[0].wait()
    loads[1].wait()
    stores = []
    for slot in range(slots):
        used, _ = held_by(me, slot, owner_smem, layer_smem)
        grad = product(
            averaged[:, slot * rank:(slot + 1) * rank], high_ref[slot], low_ref[slot], ((1,), (0,))
        )
        momentum = momentum_decay * momentum_ref[slot] + grad
        m_ref[slot] = jnp.where(used == 1, momentum, 0.0)
        loads[2 + slot].wait()
        weights = w_ref[slot] - outer_rate * (grad + momentum_decay * momentum)
        w_ref[slot] = jnp.where(used == 1, weights, 0.0)
        for which, (source, target) in enumerate(((m_ref, new_momentum_ref), (w_ref, new_weights_ref))):
            store = pltpu.make_async_copy(source.at[slot], target.at[slot], out_sems.at[slot, which])
            store.start()
            stores.append(store)
    for half in range(2):

        @pl.when(core == half)
        def _():
            for block in range(blocks):
                owner, slot = place_of(owner_smem, block)
                for part, source in ((half, near_ref), (1 - half, far_ref)):
                    here = pl.ds(part * columns, columns)
                    rows_ref[block, :, here] = (
                        source[slot, owner, :, :columns] - grad_ref[block, :, here]
                    )

    store = pltpu.make_async_copy(rows_ref, replica_ref, rows_sem)
    store.start()
    stores.append(store)
    for store in stores:
        store.wait()


def local(replica_delta, layer_basis, layer_of, owner_of, weights_owned, momentum_owned):
    own_count = lax.axis_size("own")
    rep_count = lax.axis_size("rep")
    slots, owned_rows, width = weights_owned.shape
    blocks, rows = replica_delta.shape[1:3]
    layers, _, rank = layer_basis.shape
    f32, bf16 = jnp.float32, jnp.bfloat16
    shape = jax.ShapeDtypeStruct
    across_count = rep_count // 2
    columns = width // 2
    total = columns + slots * rank
    basis = jnp.swapaxes(layer_basis, 1, 2)

    def stay(array):
        return pltpu.with_memory_space_constraint(array, pltpu.HBM)

    weights, momentum = stay(weights_owned), stay(momentum_owned)

    def swap(array, bits):
        pairs = [(rep, rep ^ bits) for rep in range(rep_count)]
        return lax.ppermute(array, "rep", pairs)

    sent, coeffs = pl.pallas_call(
        outset_kernel,
        out_shape=[
            shape((across_count, own_count, rows, total), f32),
            shape((own_count, rows, slots * rank), f32),
        ],
        in_specs=[HBM] * 6,
        out_specs=[HBM, VMEM],
        scratch_shapes=[
            pltpu.SMEM(owner_of.shape, jnp.int32),
            pltpu.SMEM(layer_of.shape, jnp.int32),
            pltpu.VMEM(replica_delta.shape[1:], f32),
            pltpu.VMEM(basis.shape, f32),
            pltpu.VMEM((owned_rows, columns), f32),
            pltpu.VMEM((owned_rows, columns), f32),
            pltpu.VMEM((own_count, rows, total), f32),
            pltpu.SemaphoreType.DMA((5 + layers,)),
            pltpu.SemaphoreType.DMA((across_count,)),
        ],
        compiler_params=params(replica_delta, basis, basis, weights_owned),
        name="outset",
    )(stay(owner_of), stay(layer_of), stay(replica_delta[0]), stay(basis), weights, momentum)
    groups = [
        [(across * 2 + core) * own_count + own for across in range(across_count) for own in range(own_count)]
        for core in range(2)
    ]
    near = lax.all_to_all(
        sent.reshape(across_count * own_count, rows, total),
        ("rep", "own"), split_axis=0, concat_axis=0, axis_index_groups=groups, tiled=True,
    ).reshape(sent.shape)
    coeffs = coeffs + swap(coeffs, 1)
    coeffs = coeffs + swap(coeffs, 2)
    grad, high, low, held = pl.pallas_call(
        lambda *refs: prepare_kernel(rep_count, *refs),
        out_shape=[
            shape((blocks, rows, width), f32),
            shape((slots, rank, width), bf16),
            shape((slots, rank, width), bf16),
            shape(momentum_owned.shape, f32),
        ],
        in_specs=[SMEM, SMEM, VMEM, HBM, HBM],
        out_specs=[VMEM] * 4,
        scratch_shapes=[
            pltpu.VMEM((blocks * rows, layers * rank), f32),
            pltpu.VMEM(basis.shape, f32),
            pltpu.SemaphoreType.DMA((slots,)),
            pltpu.SemaphoreType.DMA(()),
        ],
        compiler_params=params(basis, replica_delta, replica_delta, momentum_owned),
        name="prepare",
    )(owner_of, layer_of, coeffs, stay(basis), momentum)
    near = pl.pallas_call(
        after_kernel,
        out_shape=shape(near.shape, f32),
        in_specs=[ANY, ANY],
        out_specs=ANY,
        input_output_aliases={0: 0},
        compiler_params=params(),
        name="after",
    )(near, grad)
    far = swap(near, 1)
    new_weights, new_momentum, replica_weights = pl.pallas_call(
        lambda *refs: final_kernel(rep_count, *refs),
        out_shape=[
            shape(weights_owned.shape, f32),
            shape(weights_owned.shape, f32),
            shape((blocks, rows, width), f32),
        ],
        in_specs=[HBM, HBM] + [VMEM] * 6 + [HBM],
        out_specs=[HBM] * 3,
        scratch_shapes=[
            pltpu.SMEM(owner_of.shape, jnp.int32),
            pltpu.SMEM(layer_of.shape, jnp.int32),
            pltpu.VMEM(weights_owned.shape, f32),
            pltpu.VMEM(weights_owned.shape, f32),
            pltpu.VMEM((blocks, rows, width), f32),
            pltpu.SemaphoreType.DMA((2 + slots,)),
            pltpu.SemaphoreType.DMA((slots, 2)),
            pltpu.SemaphoreType.DMA(()),
        ],
        compiler_params=params(basis, weights_owned, weights_owned, replica_delta, replica_delta),
        name="final",
    )(stay(owner_of), stay(layer_of), near, far, high, low, held, grad, weights)
    return (new_weights, new_momentum, replica_weights)


def solution(mesh):
    placed = (
        P("rep", None, "own", None),
        P(),
        P(),
        P(),
        P("own", None, None),
        P("own", None, None),
    )
    return jax.shard_map(
        local,
        mesh=mesh,
        in_specs=placed,
        out_specs=(P("own", None, None), P("own", None, None), P(None, "own", None)),
        check_vma=False,
    )
```

```python
import math

import jax
import jax.numpy as jnp
from jax import lax
from jax.experimental import pallas as pl
from jax.experimental.pallas import tpu as pltpu
from jax.sharding import PartitionSpec as P

momentum_decay = 0.9
outer_rate = 0.7
carried = outer_rate * momentum_decay * momentum_decay
total_rate = outer_rate * (1.0 + momentum_decay)

VMEM = pl.BlockSpec(memory_space=pltpu.VMEM)
SMEM = pl.BlockSpec(memory_space=pltpu.SMEM)
HBM = pl.BlockSpec(memory_space=pltpu.HBM)
ANY = pl.BlockSpec(memory_space=pl.ANY)


def params(*arrays):
    held = sum(4 * math.prod(array.shape) for array in arrays)
    return pltpu.CompilerParams(vmem_limit_bytes=2 * held + 4 * 1024 * 1024)


def position():
    rep = lax.axis_index("rep")
    return lax.rem(rep, 2), rep // 2


def split(array):
    high = array.astype(jnp.bfloat16)
    low = (array - high.astype(jnp.float32)).astype(jnp.bfloat16)
    return high, low


def product(left, right_high, right_low, contract=((1,), (0,))):
    rows = left.shape[0]
    high, low = split(left)

    def dot(a, b):
        return lax.dot_general(
            a, b, (contract, ((), ())), preferred_element_type=jnp.float32
        )

    both = dot(jnp.concatenate([high, low], axis=0), right_high)
    return both[:rows] + (both[rows:] + dot(high, right_low))


def place_of(owner_ref, block):
    owner = owner_ref[block]
    slot = jnp.int32(0)
    for earlier in range(block):
        slot = slot + jnp.where(owner_ref[earlier] == owner, 1, 0)
    return owner, slot


def outset_kernel(
    owner_ref, layer_ref, delta_ref, basis_ref, weights_ref, momentum_ref,
    sent_ref, coeffs_ref,
    owner_smem, layer_smem, delta_vmem, basis_vmem, w_ref, m_ref, made_ref, in_sems, out_sems,
):
    owners, rows, total = sent_ref.shape
    blocks, _, width = delta_ref.shape
    layers, rank, _ = basis_ref.shape
    slots, _, window = w_ref.shape
    half = width // 2
    core, across = position()
    part = pl.ds(pl.multiple_of(core * half + across * (half - window), 128), window)
    loads = [
        pltpu.make_async_copy(source, target, in_sems.at[index])
        for index, (source, target) in enumerate((
            (weights_ref.at[:, :, part], w_ref),
            (momentum_ref.at[:, :, part], m_ref),
            (owner_ref, owner_smem),
            (layer_ref, layer_smem),
            (delta_ref, delta_vmem),
            *[(basis_ref.at[layer], basis_vmem.at[layer]) for layer in range(layers)],
        ))
    ]
    for load in loads:
        load.start()
    loads[0].wait()
    loads[1].wait()
    for owner in range(owners):
        here = pl.ds(owner * rows, rows)
        for slot in range(slots):
            made_ref[owner, :, slot * window:(slot + 1) * window] = (
                w_ref[slot, here, :] - carried * m_ref[slot, here, :]
            )
    mixed = slots * window
    early = pltpu.make_async_copy(
        made_ref.at[:, :, :mixed], sent_ref.at[:, :, :mixed], out_sems.at[0]
    )
    early.start()
    for load in loads[2:5]:
        load.wait()
    for load in loads[5:]:
        load.wait()
    high, low = split(basis_vmem[...].reshape(layers * rank, width))
    products = product(delta_vmem[...].reshape(blocks * rows, width), high, low, ((1,), (1,)))
    lane = lax.broadcasted_iota(jnp.int32, (rows, 2 * rank), 1)
    coeffs_ref[...] = jnp.zeros_like(coeffs_ref)
    for block in range(blocks):
        owner, slot = place_of(owner_smem, block)
        folded = jnp.zeros((rows, 2 * rank), jnp.float32)
        for pair in range(layers // 2):
            own = products[block * rows:(block + 1) * rows, 2 * rank * pair:2 * rank * (pair + 1)]
            folded = folded + jnp.where(2 * pair + lane // rank == layer_smem[block], own, 0.0)
        folded = folded + pltpu.roll(folded, rank, 1)
        placed = jnp.where(lane // rank == slot, folded, 0.0)
        coeffs_ref[owner] = coeffs_ref[owner] + placed
    made_ref[:, :, mixed:] = coeffs_ref[...]
    late = pltpu.make_async_copy(
        made_ref.at[:, :, mixed:], sent_ref.at[:, :, mixed:], out_sems.at[1]
    )
    late.start()
    early.wait()
    late.wait()


def held_by(me, slot, owner_ref, layer_ref):
    used, layer = jnp.int32(0), jnp.int32(0)
    for block in range(owner_ref.shape[0]):
        owner, place = place_of(owner_ref, block)
        here = (owner == me) & (place == slot)
        layer = jnp.where(here, layer_ref[block], layer)
        used = jnp.where(here, 1, used)
    return used, layer


def prepare_kernel(
    reps, owner_ref, layer_ref, coeffs_ref, basis_ref, momentum_ref,
    grad_ref, high_ref, low_ref, held_ref, wide_ref, basis_vmem, sems, basis_sem,
):
    blocks, rows, width = grad_ref.shape
    layers, rank, _ = basis_ref.shape
    slots = momentum_ref.shape[0]
    me = lax.axis_index("own")
    basis_load = pltpu.make_async_copy(basis_ref, basis_vmem, basis_sem)
    basis_load.start()
    loads = []
    for slot in range(slots):
        load = pltpu.make_async_copy(momentum_ref.at[slot], held_ref.at[slot], sems.at[slot])
        load.start()
        loads.append(load)
    lane = lax.broadcasted_iota(jnp.int32, (rows, 2 * rank), 1)
    wide_lane = lax.broadcasted_iota(jnp.int32, (rows, layers * rank), 1)
    for block in range(blocks):
        owner, slot = place_of(owner_ref, block)
        both = jnp.where(lane // rank == slot, coeffs_ref[owner], 0.0)
        both = both + pltpu.roll(both, rank, 1)
        wide = jnp.concatenate([both] * (layers // 2), axis=1)
        wide_ref[pl.ds(block * rows, rows), :] = jnp.where(
            wide_lane // rank == layer_ref[block], wide, 0.0
        )
    basis_load.wait()
    high, low = split(basis_vmem[...].reshape(layers * rank, width))
    grad = product(wide_ref[...] * (total_rate / reps), high, low)
    grad_ref[...] = grad.reshape(blocks, rows, width)
    for slot in range(slots):
        _, layer = held_by(me, slot, owner_ref, layer_ref)
        slot_high, slot_low = split(basis_vmem[layer])
        high_ref[slot] = slot_high
        low_ref[slot] = slot_low
    for load in loads:
        load.wait()


def select_kernel(owner_ref, near_ref, grad_ref, chosen_ref, partial_ref):
    window = chosen_ref.shape[-1]
    slots = (near_ref.shape[-1] - partial_ref.shape[-1]) // window
    partial_ref[...] = near_ref[:, :, slots * window:]
    for block in range(chosen_ref.shape[0]):
        owner, slot = place_of(owner_ref, block)
        for place in range(slots):

            @pl.when(slot == place)
            def _():
                chosen_ref[block] = near_ref[owner, :, place * window:(place + 1) * window]


def owner_kernel(
    reps, owner_ref, layer_ref, coeffs_ref, high_ref, low_ref, momentum_ref, weights_ref,
    new_weights_ref, new_momentum_ref,
    owner_smem, layer_smem, w_ref, m_ref, change_ref, in_sems, out_sems,
):
    slots, rows, width = weights_ref.shape
    rank = high_ref.shape[1]
    me = lax.axis_index("own")
    sources = [(owner_ref, owner_smem), (layer_ref, layer_smem)]
    sources += [(weights_ref.at[slot], w_ref.at[slot]) for slot in range(slots)]
    loads = [
        pltpu.make_async_copy(source, target, in_sems.at[index])
        for index, (source, target) in enumerate(sources)
    ]
    for load in loads:
        load.start()
    averaged = coeffs_ref[...].reshape(rows, slots * rank) * (1.0 / reps)
    loads[0].wait()
    loads[1].wait()
    stores = []

    def send(source, target, slot, which):
        store = pltpu.make_async_copy(source.at[slot], target.at[slot], out_sems.at[slot, which])
        store.start()
        stores.append(store)

    for slot in range(slots):
        used, _ = held_by(me, slot, owner_smem, layer_smem)
        grad = product(
            averaged[:, slot * rank:(slot + 1) * rank], high_ref[slot], low_ref[slot]
        )
        momentum = momentum_decay * momentum_ref[slot] + grad
        m_ref[slot] = jnp.where(used == 1, momentum, 0.0)
        send(m_ref, new_momentum_ref, slot, 0)
        change_ref[slot] = outer_rate * (grad + momentum_decay * momentum)
    for slot in range(slots):
        used, _ = held_by(me, slot, owner_smem, layer_smem)
        loads[2 + slot].wait()
        w_ref[slot] = jnp.where(used == 1, w_ref[slot] - change_ref[slot], 0.0)
        send(w_ref, new_weights_ref, slot, 1)
    for store in stores:
        store.wait()


def rows_kernel(
    near_ref, near_across_ref, far_ref, far_across_ref, grad_ref, replica_ref, rows_ref, sems
):
    window = near_ref.shape[-1]
    width = grad_ref.shape[-1]
    half = width // 2
    core, across = position()
    for near_core in range(2):
        for near_across in range(2):

            @pl.when((core == near_core) & (across == near_across))
            def _():
                stores = []
                for which, (part, sources) in enumerate((
                    (near_core, (near_ref, near_across_ref)),
                    (1 - near_core, (far_ref, far_across_ref)),
                )):
                    left, right = sources if near_across == 0 else sources[::-1]
                    start, seam, end = part * half, part * half + window, (part + 1) * half
                    rows_ref[:, :, start:seam] = left[...] - grad_ref[:, :, start:seam]
                    rows_ref[:, :, seam:end] = (
                        right[:, :, 2 * window - half:] - grad_ref[:, :, seam:end]
                    )
                    store = pltpu.make_async_copy(
                        rows_ref.at[:, :, start:end], replica_ref.at[:, :, start:end], sems.at[which]
                    )
                    store.start()
                    stores.append(store)
                for store in stores:
                    store.wait()


def local(replica_delta, layer_basis, layer_of, owner_of, weights_owned, momentum_owned):
    own_count = lax.axis_size("own")
    rep_count = lax.axis_size("rep")
    slots, owned_rows, width = weights_owned.shape
    blocks, rows = replica_delta.shape[1:3]
    layers, _, rank = layer_basis.shape
    f32, bf16 = jnp.float32, jnp.bfloat16
    shape = jax.ShapeDtypeStruct
    window = -(-width // 512) * 128
    total = slots * window + slots * rank
    basis = jnp.swapaxes(layer_basis, 1, 2)

    def stay(array):
        return pltpu.with_memory_space_constraint(array, pltpu.HBM)

    weights, momentum = stay(weights_owned), stay(momentum_owned)

    def swap(array, bits):
        pairs = [(rep, rep ^ bits) for rep in range(rep_count)]
        return lax.ppermute(array, "rep", pairs)

    sent, coeffs = pl.pallas_call(
        outset_kernel,
        out_shape=[
            shape((own_count, rows, total), f32),
            shape((own_count, rows, slots * rank), f32),
        ],
        in_specs=[HBM] * 6,
        out_specs=[HBM, VMEM],
        scratch_shapes=[
            pltpu.SMEM(owner_of.shape, jnp.int32),
            pltpu.SMEM(layer_of.shape, jnp.int32),
            pltpu.VMEM(replica_delta.shape[1:], f32),
            pltpu.VMEM(basis.shape, f32),
            pltpu.VMEM((slots, owned_rows, window), f32),
            pltpu.VMEM((slots, owned_rows, window), f32),
            pltpu.VMEM((own_count, rows, total), f32),
            pltpu.SemaphoreType.DMA((5 + layers,)),
            pltpu.SemaphoreType.DMA((2,)),
        ],
        compiler_params=params(replica_delta, basis, basis, weights_owned),
        name="outset",
    )(stay(owner_of), stay(layer_of), stay(replica_delta[0]), stay(basis), weights, momentum)
    near = lax.all_to_all(sent, "own", split_axis=0, concat_axis=0, tiled=True)

    coeffs = coeffs + swap(coeffs, 1)
    coeffs = coeffs + swap(coeffs, 2)
    grad, high, low, held = pl.pallas_call(
        lambda *refs: prepare_kernel(rep_count, *refs),
        out_shape=[
            shape((blocks, rows, width), f32),
            shape((slots, rank, width), bf16),
            shape((slots, rank, width), bf16),
            shape(momentum_owned.shape, f32),
        ],
        in_specs=[SMEM, SMEM, VMEM, HBM, HBM],
        out_specs=[VMEM] * 4,
        scratch_shapes=[
            pltpu.VMEM((blocks * rows, layers * rank), f32),
            pltpu.VMEM(basis.shape, f32),
            pltpu.SemaphoreType.DMA((slots,)),
            pltpu.SemaphoreType.DMA(()),
        ],
        compiler_params=params(basis, replica_delta, replica_delta, momentum_owned),
        name="prepare",
    )(owner_of, layer_of, coeffs, stay(basis), momentum)

    chosen, partial = pl.pallas_call(
        select_kernel,
        out_shape=[
            shape((blocks, rows, window), f32),
            shape((own_count, rows, slots * rank), f32),
        ],
        in_specs=[SMEM, VMEM, ANY],
        out_specs=[VMEM, VMEM],
        compiler_params=params(near, near),
        name="select",
    )(owner_of, near, grad)
    chosen_across = swap(chosen, 2)
    far = swap(chosen, 1)
    partial = (partial + swap(partial, 1)) + (swap(partial, 2) + swap(partial, 3))
    far_across = swap(chosen_across, 1)
    new_weights, new_momentum = pl.pallas_call(
        lambda *refs: owner_kernel(rep_count, *refs),
        out_shape=[shape(weights_owned.shape, f32)] * 2,
        in_specs=[HBM, HBM] + [VMEM] * 4 + [HBM],
        out_specs=[HBM] * 2,
        scratch_shapes=[
            pltpu.SMEM(owner_of.shape, jnp.int32),
            pltpu.SMEM(layer_of.shape, jnp.int32),
            pltpu.VMEM(weights_owned.shape, f32),
            pltpu.VMEM(weights_owned.shape, f32),
            pltpu.VMEM(weights_owned.shape, f32),
            pltpu.SemaphoreType.DMA((2 + slots,)),
            pltpu.SemaphoreType.DMA((slots, 2)),
        ],
        compiler_params=params(basis, weights_owned, weights_owned, weights_owned),
        name="owner",
    )(stay(owner_of), stay(layer_of), partial, high, low, held, weights)
    replica_weights = pl.pallas_call(
        rows_kernel,
        out_shape=shape((blocks, rows, width), f32),
        in_specs=[VMEM] * 5,
        out_specs=HBM,
        scratch_shapes=[pltpu.VMEM((blocks, rows, width), f32), pltpu.SemaphoreType.DMA((2,))],
        compiler_params=params(replica_delta, replica_delta, replica_delta),
        name="rows",
    )(chosen, chosen_across, far, far_across, grad)
    return (new_weights, new_momentum, replica_weights)


def solution(mesh):
    placed = (
        P("rep", None, "own", None),
        P(),
        P(),
        P(),
        P("own", None, None),
        P("own", None, None),
    )
    return jax.shard_map(
        local,
        mesh=mesh,
        in_specs=placed,
        out_specs=(P("own", None, None), P("own", None, None), P(None, "own", None)),
        check_vma=False,
    )
```

```python
import math

import jax
import jax.numpy as jnp
from jax import lax
from jax.experimental import pallas as pl
from jax.experimental.pallas import tpu as pltpu
from jax.sharding import PartitionSpec as P

momentum_decay = 0.9
outer_rate = 0.7
carried = outer_rate * momentum_decay * momentum_decay
total_rate = outer_rate * (1.0 + momentum_decay)

VMEM = pl.BlockSpec(memory_space=pltpu.VMEM)
SMEM = pl.BlockSpec(memory_space=pltpu.SMEM)
HBM = pl.BlockSpec(memory_space=pltpu.HBM)
ANY = pl.BlockSpec(memory_space=pl.ANY)


def params(*arrays):
    held = sum(4 * math.prod(array.shape) for array in arrays)
    return pltpu.CompilerParams(vmem_limit_bytes=2 * held + 4 * 1024 * 1024)


def position():
    rep = lax.axis_index("rep")
    return lax.rem(rep, 2), rep // 2


def split(array):
    high = array.astype(jnp.bfloat16)
    low = (array - high.astype(jnp.float32)).astype(jnp.bfloat16)
    return high, low


def product(left, right_high, right_low, contract=((1,), (0,))):
    rows = left.shape[0]
    high, low = split(left)

    def dot(a, b):
        return lax.dot_general(
            a, b, (contract, ((), ())), preferred_element_type=jnp.float32
        )

    both = dot(jnp.concatenate([high, low], axis=0), right_high)
    return both[:rows] + (both[rows:] + dot(high, right_low))


def place_of(owner_ref, block):
    owner = owner_ref[block]
    slot = jnp.int32(0)
    for earlier in range(block):
        slot = slot + jnp.where(owner_ref[earlier] == owner, 1, 0)
    return owner, slot


def outset_kernel(
    owner_ref, layer_ref, delta_ref, basis_ref, weights_ref, momentum_ref,
    sent_ref, coeffs_ref,
    owner_smem, layer_smem, delta_vmem, basis_vmem, high_ref, low_ref, w_ref, m_ref, made_ref,
    in_sems, out_sems,
):
    owners, rows, total = sent_ref.shape
    blocks, _, width = delta_ref.shape
    layers, rank, _ = basis_ref.shape
    slots, _, window = w_ref.shape
    half = width // 2
    core, across = position()
    part = pl.ds(pl.multiple_of(core * half + across * (half - window), 128), window)
    loads = [
        pltpu.make_async_copy(source, target, in_sems.at[index])
        for index, (source, target) in enumerate((
            (weights_ref.at[:, :, part], w_ref),
            (momentum_ref.at[:, :, part], m_ref),
            (owner_ref, owner_smem),
            (layer_ref, layer_smem),
            (delta_ref, delta_vmem),
            *[(basis_ref.at[layer], basis_vmem.at[layer]) for layer in range(layers)],
        ))
    ]
    for load in loads:
        load.start()
    loads[0].wait()
    loads[1].wait()
    for owner in range(owners):
        here = pl.ds(owner * rows, rows)
        for slot in range(slots):
            made_ref[owner, :, slot * window:(slot + 1) * window] = (
                w_ref[slot, here, :] - carried * m_ref[slot, here, :]
            )
    mixed = slots * window
    early = pltpu.make_async_copy(
        made_ref.at[:, :, :mixed], sent_ref.at[:, :, :mixed], out_sems.at[0]
    )
    early.start()
    for layer in range(layers):
        loads[5 + layer].wait()
        here = pl.ds(layer * rank, rank)
        high_ref[here, :], low_ref[here, :] = split(basis_vmem[layer])
    for load in loads[2:5]:
        load.wait()
    products = product(
        delta_vmem[...].reshape(blocks * rows, width), high_ref[...], low_ref[...], ((1,), (1,))
    )
    lane = lax.broadcasted_iota(jnp.int32, (rows, 2 * rank), 1)
    coeffs_ref[...] = jnp.zeros_like(coeffs_ref)
    for block in range(blocks):
        owner, slot = place_of(owner_smem, block)
        folded = jnp.zeros((rows, 2 * rank), jnp.float32)
        for pair in range(layers // 2):
            own = products[block * rows:(block + 1) * rows, 2 * rank * pair:2 * rank * (pair + 1)]
            folded = folded + jnp.where(2 * pair + lane // rank == layer_smem[block], own, 0.0)
        folded = folded + pltpu.roll(folded, rank, 1)
        placed = jnp.where(lane // rank == slot, folded, 0.0)
        coeffs_ref[owner] = coeffs_ref[owner] + placed
    made_ref[:, :, mixed:] = coeffs_ref[...]
    late = pltpu.make_async_copy(
        made_ref.at[:, :, mixed:], sent_ref.at[:, :, mixed:], out_sems.at[1]
    )
    late.start()
    early.wait()
    late.wait()


def held_by(me, slot, owner_ref, layer_ref):
    used, layer = jnp.int32(0), jnp.int32(0)
    for block in range(owner_ref.shape[0]):
        owner, place = place_of(owner_ref, block)
        here = (owner == me) & (place == slot)
        layer = jnp.where(here, layer_ref[block], layer)
        used = jnp.where(here, 1, used)
    return used, layer


def prepare_kernel(
    reps, owner_ref, layer_ref, coeffs_ref, basis_ref, momentum_ref,
    grad_ref, high_ref, low_ref, held_ref, marks_ref,
    wide_ref, basis_vmem, slot_vmem, sems,
):
    blocks, rows, window = grad_ref.shape
    layers, rank, width = basis_ref.shape
    slots = momentum_ref.shape[0]
    places = coeffs_ref.shape[0] * slots
    half = width // 2
    me = lax.axis_index("own")
    core, across = position()
    part = pl.ds(pl.multiple_of(core * half + across * (half - window), 128), window)
    found = [held_by(me, slot, owner_ref, layer_ref) for slot in range(slots)]
    loads = [pltpu.make_async_copy(basis_ref.at[:, :, part], basis_vmem, sems.at[0])]
    for slot in range(slots):
        loads.append(
            pltpu.make_async_copy(basis_ref.at[found[slot][1]], slot_vmem.at[slot], sems.at[1 + slot])
        )
    loads.append(pltpu.make_async_copy(momentum_ref, held_ref, sems.at[1 + slots]))
    for load in loads:
        load.start()
    lane = lax.broadcasted_iota(jnp.int32, (rows, 2 * rank), 1)
    wide_lane = lax.broadcasted_iota(jnp.int32, (rows, layers * rank), 1)
    place_row = lax.broadcasted_iota(jnp.int32, (places, marks_ref.shape[1]), 0)
    for block in range(blocks):
        owner, slot = place_of(owner_ref, block)
        both = jnp.where(lane // rank == slot, coeffs_ref[owner], 0.0)
        both = both + pltpu.roll(both, rank, 1)
        wide = jnp.concatenate([both] * (layers // 2), axis=1)
        wide_ref[pl.ds(block * rows, rows), :] = jnp.where(
            wide_lane // rank == layer_ref[block], wide, 0.0
        )
        marks_ref[pl.ds(block * places, places), :] = jnp.where(
            place_row == owner * slots + slot, 1.0, 0.0
        )
    loads[0].wait()
    high, low = split(basis_vmem[...].reshape(layers * rank, window))
    grad = product(wide_ref[...] * (total_rate / reps), high, low)
    grad_ref[...] = grad.reshape(blocks, rows, window)
    for slot in range(slots):
        loads[1 + slot].wait()
        slot_high, slot_low = split(slot_vmem[slot])
        high_ref[slot] = slot_high
        low_ref[slot] = slot_low
    loads[-1].wait()


def select_kernel(near_ref, grad_ref, marks_ref, chosen_ref, given_ref):
    blocks, rows, window = chosen_ref.shape
    owners = near_ref.shape[0]
    slots = near_ref.shape[-1] // window
    places = owners * slots
    rest = given_ref.shape[-1]
    lanes = marks_ref.shape[1]
    _, across = position()

    def one(block, carry):
        total = -grad_ref[block]
        for owner in range(owners):
            for slot in range(slots):
                mark = marks_ref[pl.ds(block * places + owner * slots + slot, 1), :]
                mark = jnp.concatenate([mark] * (window // lanes), axis=1)
                total = total + mark * near_ref[owner, :, slot * window:(slot + 1) * window]
        chosen_ref[block] = total
        return carry

    lax.fori_loop(0, blocks, one, 0, unroll=blocks <= 8)
    for side in range(2):

        @pl.when(across == side)
        def _():
            first = side * (window - rest)
            given_ref[...] = chosen_ref[:, :, first:first + rest]


def after_kernel(rows_ref, done_ref, same_ref):
    pass


def final_kernel(
    reps, owner_ref, layer_ref, coeffs_ref, high_ref, low_ref, momentum_ref,
    near_ref, near_rest_ref, far_ref, far_rest_ref, weights_ref,
    new_weights_ref, new_momentum_ref, replica_ref,
    owner_smem, layer_smem, w_ref, m_ref, change_ref, in_sems, out_sems, rows_sems,
):
    slots, rows, width = weights_ref.shape
    rank = high_ref.shape[1]
    window, rest = near_ref.shape[-1], near_rest_ref.shape[-1]
    half = window + rest
    me = lax.axis_index("own")
    core, across = position()
    sources = [(owner_ref, owner_smem), (layer_ref, layer_smem)]
    sources += [(weights_ref.at[slot], w_ref.at[slot]) for slot in range(slots)]
    loads = [
        pltpu.make_async_copy(source, target, in_sems.at[index])
        for index, (source, target) in enumerate(sources)
    ]
    for load in loads:
        load.start()
    stores = []
    for which, (side, whole, other) in enumerate((
        (core, near_ref, near_rest_ref), (1 - core, far_ref, far_rest_ref),
    )):
        for index, (source, first) in enumerate((
            (whole, side * half + across * rest),
            (other, side * half + (1 - across) * window),
        )):
            here = pl.ds(pl.multiple_of(first, 128), source.shape[-1])
            store = pltpu.make_async_copy(
                source, replica_ref.at[:, :, here], rows_sems.at[which, index]
            )
            store.start()
            stores.append(store)
    averaged = coeffs_ref[...].reshape(rows, slots * rank) * (1.0 / reps)
    loads[0].wait()
    loads[1].wait()
    used = [held_by(me, slot, owner_smem, layer_smem)[0] for slot in range(slots)]

    def send(source, target, slot, which):
        store = pltpu.make_async_copy(source.at[slot], target.at[slot], out_sems.at[slot, which])
        store.start()
        stores.append(store)

    for slot in range(slots):
        grad = product(
            averaged[:, slot * rank:(slot + 1) * rank], high_ref[slot], low_ref[slot]
        )
        momentum = momentum_decay * momentum_ref[slot] + grad
        m_ref[slot] = jnp.where(used[slot] == 1, momentum, 0.0)
        send(m_ref, new_momentum_ref, slot, 0)
        change_ref[slot] = outer_rate * (grad + momentum_decay * momentum)
    for slot in range(slots):
        loads[2 + slot].wait()
        w_ref[slot] = jnp.where(used[slot] == 1, w_ref[slot] - change_ref[slot], 0.0)
        send(w_ref, new_weights_ref, slot, 1)
    for store in stores:
        store.wait()


def local(replica_delta, layer_basis, layer_of, owner_of, weights_owned, momentum_owned):
    own_count = lax.axis_size("own")
    rep_count = lax.axis_size("rep")
    slots, owned_rows, width = weights_owned.shape
    blocks, rows = replica_delta.shape[1:3]
    layers, _, rank = layer_basis.shape
    f32, bf16 = jnp.float32, jnp.bfloat16
    shape = jax.ShapeDtypeStruct
    window = -(-width // 512) * 128
    rest = width // 2 - window
    total = slots * window + slots * rank
    basis = jnp.swapaxes(layer_basis, 1, 2)

    def stay(array):
        return pltpu.with_memory_space_constraint(array, pltpu.HBM)

    weights, momentum = stay(weights_owned), stay(momentum_owned)

    def swap(array, bits):
        pairs = [(rep, rep ^ bits) for rep in range(rep_count)]
        return lax.ppermute(array, "rep", pairs)

    sent, coeffs = pl.pallas_call(
        outset_kernel,
        out_shape=[
            shape((own_count, rows, total), f32),
            shape((own_count, rows, slots * rank), f32),
        ],
        in_specs=[HBM] * 6,
        out_specs=[HBM, VMEM],
        scratch_shapes=[
            pltpu.SMEM(owner_of.shape, jnp.int32),
            pltpu.SMEM(layer_of.shape, jnp.int32),
            pltpu.VMEM(replica_delta.shape[1:], f32),
            pltpu.VMEM(basis.shape, f32),
            pltpu.VMEM((layers * rank, width), bf16),
            pltpu.VMEM((layers * rank, width), bf16),
            pltpu.VMEM((slots, owned_rows, window), f32),
            pltpu.VMEM((slots, owned_rows, window), f32),
            pltpu.VMEM((own_count, rows, total), f32),
            pltpu.SemaphoreType.DMA((5 + layers,)),
            pltpu.SemaphoreType.DMA((2,)),
        ],
        compiler_params=params(replica_delta, basis, basis, weights_owned),
        name="outset",
    )(stay(owner_of), stay(layer_of), stay(replica_delta[0]), stay(basis), weights, momentum)
    near = lax.all_to_all(sent, "own", split_axis=0, concat_axis=0, tiled=True)

    coeffs = coeffs + swap(coeffs, 1)
    coeffs = coeffs + swap(coeffs, 2)
    grad, high, low, held, marks = pl.pallas_call(
        lambda *refs: prepare_kernel(rep_count, *refs),
        out_shape=[
            shape((blocks, rows, window), f32),
            shape((slots, rank, width), bf16),
            shape((slots, rank, width), bf16),
            shape(momentum_owned.shape, f32),
            shape((blocks * own_count * slots, 128), f32),
        ],
        in_specs=[SMEM, SMEM, VMEM, HBM, HBM],
        out_specs=[VMEM] * 5,
        scratch_shapes=[
            pltpu.VMEM((blocks * rows, layers * rank), f32),
            pltpu.VMEM((layers, rank, window), f32),
            pltpu.VMEM((slots, rank, width), f32),
            pltpu.SemaphoreType.DMA((2 + slots,)),
        ],
        compiler_params=params(basis, replica_delta, replica_delta, momentum_owned),
        name="prepare",
    )(owner_of, layer_of, coeffs, stay(basis), momentum)

    def after(array, done):
        return pl.pallas_call(
            after_kernel,
            out_shape=shape(array.shape, f32),
            in_specs=[ANY, ANY],
            out_specs=ANY,
            input_output_aliases={0: 0},
            compiler_params=params(),
            name="after",
        )(array, done)

    near = after(near, grad)
    partial = near[:, :, slots * window:]
    partial = (partial + swap(partial, 1)) + (swap(partial, 2) + swap(partial, 3))
    chosen, given = pl.pallas_call(
        select_kernel,
        out_shape=[
            shape((blocks, rows, window), f32),
            shape((blocks, rows, rest), f32),
        ],
        in_specs=[VMEM] * 3,
        out_specs=[VMEM] * 2,
        compiler_params=params(near, near, marks),
        name="select",
    )(near, grad, marks)
    far = swap(chosen, 1)
    near_rest = swap(given, 2)
    far_rest = swap(near_rest, 1)
    new_weights, new_momentum, replica_weights = pl.pallas_call(
        lambda *refs: final_kernel(rep_count, *refs),
        out_shape=[
            shape(weights_owned.shape, f32),
            shape(weights_owned.shape, f32),
            shape((blocks, rows, width), f32),
        ],
        in_specs=[HBM, HBM] + [VMEM] * 8 + [HBM],
        out_specs=[HBM] * 3,
        scratch_shapes=[
            pltpu.SMEM(owner_of.shape, jnp.int32),
            pltpu.SMEM(layer_of.shape, jnp.int32),
            pltpu.VMEM(weights_owned.shape, f32),
            pltpu.VMEM(weights_owned.shape, f32),
            pltpu.VMEM(weights_owned.shape, f32),
            pltpu.SemaphoreType.DMA((2 + slots,)),
            pltpu.SemaphoreType.DMA((slots, 2)),
            pltpu.SemaphoreType.DMA((2, 2)),
        ],
        compiler_params=params(basis, weights_owned, weights_owned, weights_owned),
        name="final",
    )(
        stay(owner_of), stay(layer_of), partial, high, low, held,
        chosen, near_rest, far, far_rest, weights,
    )
    return (new_weights, new_momentum, replica_weights)


def solution(mesh):
    placed = (
        P("rep", None, "own", None),
        P(),
        P(),
        P(),
        P("own", None, None),
        P("own", None, None),
    )
    return jax.shard_map(
        local,
        mesh=mesh,
        in_specs=placed,
        out_specs=(P("own", None, None), P("own", None, None), P(None, "own", None)),
        check_vma=False,
    )
```

```python
import math

import jax
import jax.numpy as jnp
from jax import lax
from jax.experimental import pallas as pl
from jax.experimental.pallas import tpu as pltpu
from jax.sharding import PartitionSpec as P

momentum_decay = 0.9
outer_rate = 0.7
carried = outer_rate * momentum_decay * momentum_decay
total_rate = outer_rate * (1.0 + momentum_decay)

VMEM = pl.BlockSpec(memory_space=pltpu.VMEM)
SMEM = pl.BlockSpec(memory_space=pltpu.SMEM)
HBM = pl.BlockSpec(memory_space=pltpu.HBM)
ANY = pl.BlockSpec(memory_space=pl.ANY)


def params(*arrays):
    held = sum(4 * math.prod(array.shape) for array in arrays)
    return pltpu.CompilerParams(vmem_limit_bytes=2 * held + 4 * 1024 * 1024)


def position():
    rep = lax.axis_index("rep")
    return lax.rem(rep, 2), rep // 2


def split(array):
    high = array.astype(jnp.bfloat16)
    low = (array - high.astype(jnp.float32)).astype(jnp.bfloat16)
    return high, low


def product(left, right_high, right_low, contract=((1,), (0,))):
    rows = left.shape[0]
    high, low = split(left)

    def dot(a, b):
        return lax.dot_general(
            a, b, (contract, ((), ())), preferred_element_type=jnp.float32
        )

    both = dot(jnp.concatenate([high, low], axis=0), right_high)
    return both[:rows] + (both[rows:] + dot(high, right_low))


def place_of(owner_ref, block):
    owner = owner_ref[block]
    slot = jnp.int32(0)
    for earlier in range(block):
        slot = slot + jnp.where(owner_ref[earlier] == owner, 1, 0)
    return owner, slot


def outset_kernel(
    owner_ref, layer_ref, delta_ref, basis_ref, weights_ref, momentum_ref,
    sent_ref, coeffs_ref,
    owner_smem, layer_smem, delta_vmem, basis_vmem, w_ref, m_ref, made_ref, in_sems, out_sems,
):
    owners, rows, total = sent_ref.shape
    blocks, _, width = delta_ref.shape
    layers, rank, _ = basis_ref.shape
    columns = width // 2
    core, across = position()
    part = pl.ds(pl.multiple_of(core * columns, 128), columns)
    loads = [
        pltpu.make_async_copy(source, target, in_sems.at[index])
        for index, (source, target) in enumerate((
            (owner_ref, owner_smem),
            (layer_ref, layer_smem),
            (delta_ref, delta_vmem),
            *[(basis_ref.at[layer], basis_vmem.at[layer]) for layer in range(layers)],
            (weights_ref.at[:, :, part], w_ref),
            (momentum_ref.at[:, :, part], m_ref),
        ))
    ]
    for load in loads:
        load.start()
    for load in loads[2:-2]:
        load.wait()
    high, low = split(basis_vmem[...].reshape(layers * rank, width))
    products = product(delta_vmem[...].reshape(blocks * rows, width), high, low, ((1,), (1,)))
    loads[-2].wait()
    loads[-1].wait()
    upper = lax.broadcasted_iota(jnp.int32, (rows, columns), 0) < rows // 2
    for owner in range(owners):
        here = pl.ds(owner * rows, rows)
        first, second = [
            w_ref[slot, here, :] - carried * m_ref[slot, here, :] for slot in range(2)
        ]
        for side in range(2):

            @pl.when(across == side)
            def _():
                if side == 0:
                    tile = jnp.where(upper, first, pltpu.roll(second, rows // 2, 0))
                else:
                    tile = jnp.where(upper, pltpu.roll(first, rows // 2, 0), second)
                made_ref[owner, :, :columns] = tile
    early = pltpu.make_async_copy(
        made_ref.at[:, :, :columns], sent_ref.at[:, :, :columns], out_sems.at[0]
    )
    early.start()
    loads[0].wait()
    loads[1].wait()
    lane = lax.broadcasted_iota(jnp.int32, (rows, 2 * rank), 1)
    coeffs_ref[...] = jnp.zeros_like(coeffs_ref)
    for block in range(blocks):
        owner, slot = place_of(owner_smem, block)
        folded = jnp.zeros((rows, 2 * rank), jnp.float32)
        for pair in range(layers // 2):
            own = products[block * rows:(block + 1) * rows, 2 * rank * pair:2 * rank * (pair + 1)]
            folded = folded + jnp.where(2 * pair + lane // rank == layer_smem[block], own, 0.0)
        folded = folded + pltpu.roll(folded, rank, 1)
        placed = jnp.where(lane // rank == slot, folded, 0.0)
        coeffs_ref[owner] = coeffs_ref[owner] + placed
    made_ref[:, :, columns:] = coeffs_ref[...]
    late = pltpu.make_async_copy(
        made_ref.at[:, :, columns:], sent_ref.at[:, :, columns:], out_sems.at[1]
    )
    late.start()
    early.wait()
    late.wait()


def held_by(me, slot, owner_ref, layer_ref):
    used, layer = jnp.int32(0), jnp.int32(0)
    for block in range(owner_ref.shape[0]):
        owner, place = place_of(owner_ref, block)
        here = (owner == me) & (place == slot)
        layer = jnp.where(here, layer_ref[block], layer)
        used = jnp.where(here, 1, used)
    return used, layer


def prepare_kernel(
    reps, owner_ref, layer_ref, coeffs_ref, basis_ref, momentum_ref, weights_ref,
    grad_ref, high_ref, low_ref, held_ref, first_ref, marks_ref,
    wide_ref, basis_vmem, slot_vmem, sems,
):
    pairs, rows, columns = grad_ref.shape
    blocks = owner_ref.shape[0]
    layers, rank, width = basis_ref.shape
    slots = momentum_ref.shape[0]
    places = coeffs_ref.shape[0] * slots
    me = lax.axis_index("own")
    core, across = position()
    part = pl.ds(pl.multiple_of(core * columns, 128), columns)
    found = [held_by(me, slot, owner_ref, layer_ref) for slot in range(slots)]
    loads = [pltpu.make_async_copy(basis_ref.at[:, :, part], basis_vmem, sems.at[0])]
    for slot in range(slots):
        loads.append(
            pltpu.make_async_copy(basis_ref.at[found[slot][1]], slot_vmem.at[slot], sems.at[1 + slot])
        )
    loads.append(pltpu.make_async_copy(momentum_ref, held_ref, sems.at[1 + slots]))
    loads.append(pltpu.make_async_copy(weights_ref.at[0], first_ref, sems.at[2 + slots]))
    for load in loads:
        load.start()
    lane = lax.broadcasted_iota(jnp.int32, (rows, 2 * rank), 1)
    wide_lane = lax.broadcasted_iota(jnp.int32, (rows, layers * rank), 1)
    place_row = lax.broadcasted_iota(jnp.int32, (places, marks_ref.shape[1]), 0)
    upper = lax.broadcasted_iota(jnp.int32, (rows, layers * rank), 0) < rows // 2
    for pair in range(pairs):
        parts = []
        for odd in range(2):
            block = 2 * pair + odd
            owner, slot = place_of(owner_ref, block)
            both = jnp.where(lane // rank == slot, coeffs_ref[owner], 0.0)
            both = both + pltpu.roll(both, rank, 1)
            wide = jnp.concatenate([both] * (layers // 2), axis=1)
            wide = jnp.where(wide_lane // rank == layer_ref[block], wide, 0.0)
            parts.append(jnp.where(across == odd, wide, pltpu.roll(wide, rows // 2, 0)))
            marks_ref[pl.ds(block * places, places), :] = jnp.where(
                place_row == owner * slots + slot, 1.0, 0.0
            )
        wide_ref[pl.ds(pair * rows, rows), :] = jnp.where(upper, parts[0], parts[1])
    loads[0].wait()
    high, low = split(basis_vmem[...].reshape(layers * rank, columns))
    grad = product(wide_ref[...] * (total_rate / reps), high, low)
    grad_ref[...] = grad.reshape(pairs, rows, columns)
    for slot in range(slots):
        loads[1 + slot].wait()
        slot_high, slot_low = split(slot_vmem[slot])
        high_ref[slot] = slot_high
        low_ref[slot] = slot_low
    loads[-2].wait()
    loads[-1].wait()


def select_kernel(near_ref, grad_ref, marks_ref, chosen_ref):
    pairs, rows, columns = chosen_ref.shape
    owners = near_ref.shape[0]
    lanes = marks_ref.shape[1]
    upper = lax.broadcasted_iota(jnp.int32, (rows, columns), 0) < rows // 2

    def one(pair, carry):
        parts = []
        for odd in range(2):
            first = (2 * pair + odd) * 2 * owners
            sums = []
            for slot in range(2):
                total = jnp.zeros((rows, columns), jnp.float32)
                for owner in range(owners):
                    mark = marks_ref[pl.ds(first + 2 * owner + slot, 1), :]
                    mark = jnp.concatenate([mark] * (columns // lanes), axis=1)
                    total = total + mark * near_ref[owner, :, :columns]
                sums.append(total)
            parts.append(sums[odd] + pltpu.roll(sums[1 - odd], rows // 2, 0))
        chosen_ref[pair] = jnp.where(upper, parts[0], parts[1]) - grad_ref[pair]
        return carry

    lax.fori_loop(0, pairs, one, 0, unroll=pairs <= 4)


def after_kernel(rows_ref, done_ref, same_ref):
    pass


def final_kernel(
    reps, owner_ref, layer_ref, coeffs_ref, high_ref, low_ref, momentum_ref, first_ref,
    near_ref, near_across_ref, far_ref, far_across_ref, weights_ref,
    new_weights_ref, new_momentum_ref, replica_ref,
    owner_smem, layer_smem, w_ref, m_ref, change_ref, rows_ref, in_sems, out_sems, rows_sem,
):
    slots, rows, width = weights_ref.shape
    rank = high_ref.shape[1]
    pairs, tile, columns = near_ref.shape
    me = lax.axis_index("own")
    core, across = position()
    sources = [(owner_ref, owner_smem), (layer_ref, layer_smem)]
    sources += [(weights_ref.at[slot], w_ref.at[slot]) for slot in range(1, slots)]
    loads = [
        pltpu.make_async_copy(source, target, in_sems.at[index])
        for index, (source, target) in enumerate(sources)
    ]
    for load in loads:
        load.start()
    upper = lax.broadcasted_iota(jnp.int32, (tile, columns), 0) < tile // 2
    for near_core in range(2):
        for near_across in range(2):

            @pl.when((core == near_core) & (across == near_across))
            def _():
                for side, sources in (
                    (near_core, (near_ref, near_across_ref)),
                    (1 - near_core, (far_ref, far_across_ref)),
                ):
                    top, bottom = sources if near_across == 0 else sources[::-1]
                    here = pl.ds(side * columns, columns)
                    for pair in range(pairs):
                        above, below = top[pair], bottom[pair]
                        rows_ref[2 * pair, :, here] = jnp.where(
                            upper, above, pltpu.roll(below, tile // 2, 0)
                        )
                        rows_ref[2 * pair + 1, :, here] = jnp.where(
                            upper, pltpu.roll(above, tile // 2, 0), below
                        )

    store = pltpu.make_async_copy(rows_ref, replica_ref, rows_sem)
    store.start()
    stores = [store]
    averaged = coeffs_ref[...].reshape(rows, slots * rank) * (1.0 / reps)
    loads[0].wait()
    loads[1].wait()
    used = [held_by(me, slot, owner_smem, layer_smem)[0] for slot in range(slots)]

    def send(source, target, slot, which):
        store = pltpu.make_async_copy(source.at[slot], target.at[slot], out_sems.at[slot, which])
        store.start()
        stores.append(store)

    for slot in range(slots):
        grad = product(
            averaged[:, slot * rank:(slot + 1) * rank], high_ref[slot], low_ref[slot]
        )
        momentum = momentum_decay * momentum_ref[slot] + grad
        m_ref[slot] = jnp.where(used[slot] == 1, momentum, 0.0)
        send(m_ref, new_momentum_ref, slot, 0)
        change = outer_rate * (grad + momentum_decay * momentum)
        if slot == 0:
            w_ref[0] = jnp.where(used[0] == 1, first_ref[...] - change, 0.0)
            send(w_ref, new_weights_ref, 0, 1)
        else:
            change_ref[slot] = change
    for slot in range(1, slots):
        loads[1 + slot].wait()
        w_ref[slot] = jnp.where(used[slot] == 1, w_ref[slot] - change_ref[slot], 0.0)
        send(w_ref, new_weights_ref, slot, 1)
    for store in stores:
        store.wait()


def local(replica_delta, layer_basis, layer_of, owner_of, weights_owned, momentum_owned):
    own_count = lax.axis_size("own")
    rep_count = lax.axis_size("rep")
    slots, owned_rows, width = weights_owned.shape
    blocks, rows = replica_delta.shape[1:3]
    layers, _, rank = layer_basis.shape
    f32, bf16 = jnp.float32, jnp.bfloat16
    shape = jax.ShapeDtypeStruct
    columns = width // 2
    total = columns + slots * rank
    basis = jnp.swapaxes(layer_basis, 1, 2)

    def stay(array):
        return pltpu.with_memory_space_constraint(array, pltpu.HBM)

    weights, momentum = stay(weights_owned), stay(momentum_owned)

    def swap(array, bits):
        pairs = [(rep, rep ^ bits) for rep in range(rep_count)]
        return lax.ppermute(array, "rep", pairs)

    sent, coeffs = pl.pallas_call(
        outset_kernel,
        out_shape=[
            shape((own_count, rows, total), f32),
            shape((own_count, rows, slots * rank), f32),
        ],
        in_specs=[HBM] * 6,
        out_specs=[HBM, VMEM],
        scratch_shapes=[
            pltpu.SMEM(owner_of.shape, jnp.int32),
            pltpu.SMEM(layer_of.shape, jnp.int32),
            pltpu.VMEM(replica_delta.shape[1:], f32),
            pltpu.VMEM(basis.shape, f32),
            pltpu.VMEM((slots, owned_rows, columns), f32),
            pltpu.VMEM((slots, owned_rows, columns), f32),
            pltpu.VMEM((own_count, rows, total), f32),
            pltpu.SemaphoreType.DMA((5 + layers,)),
            pltpu.SemaphoreType.DMA((2,)),
        ],
        compiler_params=params(replica_delta, basis, basis, weights_owned),
        name="outset",
    )(stay(owner_of), stay(layer_of), stay(replica_delta[0]), stay(basis), weights, momentum)
    near = lax.all_to_all(sent, "own", split_axis=0, concat_axis=0, tiled=True)

    coeffs = coeffs + swap(coeffs, 1)
    coeffs = coeffs + swap(coeffs, 2)
    grad, high, low, held, first, marks = pl.pallas_call(
        lambda *refs: prepare_kernel(rep_count, *refs),
        out_shape=[
            shape((blocks // 2, rows, columns), f32),
            shape((slots, rank, width), bf16),
            shape((slots, rank, width), bf16),
            shape(momentum_owned.shape, f32),
            shape(weights_owned.shape[1:], f32),
            shape((blocks * own_count * slots, 128), f32),
        ],
        in_specs=[SMEM, SMEM, VMEM, HBM, HBM, HBM],
        out_specs=[VMEM] * 6,
        scratch_shapes=[
            pltpu.VMEM((blocks // 2 * rows, layers * rank), f32),
            pltpu.VMEM((layers, rank, columns), f32),
            pltpu.VMEM((slots, rank, width), f32),
            pltpu.SemaphoreType.DMA((3 + slots,)),
        ],
        compiler_params=params(basis, replica_delta, replica_delta, momentum_owned, momentum_owned),
        name="prepare",
    )(owner_of, layer_of, coeffs, stay(basis), momentum, weights)

    def after(array, done):
        return pl.pallas_call(
            after_kernel,
            out_shape=shape(array.shape, f32),
            in_specs=[ANY, ANY],
            out_specs=ANY,
            input_output_aliases={0: 0},
            compiler_params=params(),
            name="after",
        )(array, done)

    near = after(near, grad)
    partial = near[:, :, columns:]
    partial = (partial + swap(partial, 1)) + (swap(partial, 2) + swap(partial, 3))
    chosen = pl.pallas_call(
        select_kernel,
        out_shape=shape((blocks // 2, rows, columns), f32),
        in_specs=[VMEM] * 3,
        out_specs=VMEM,
        compiler_params=params(near, near, marks),
        name="select",
    )(near, grad, marks)
    far = swap(chosen, 1)
    near_across = swap(chosen, 2)
    far_across = swap(near_across, 1)
    new_weights, new_momentum, replica_weights = pl.pallas_call(
        lambda *refs: final_kernel(rep_count, *refs),
        out_shape=[
            shape(weights_owned.shape, f32),
            shape(weights_owned.shape, f32),
            shape((blocks, rows, width), f32),
        ],
        in_specs=[HBM, HBM] + [VMEM] * 9 + [HBM],
        out_specs=[HBM] * 3,
        scratch_shapes=[
            pltpu.SMEM(owner_of.shape, jnp.int32),
            pltpu.SMEM(layer_of.shape, jnp.int32),
            pltpu.VMEM(weights_owned.shape, f32),
            pltpu.VMEM(weights_owned.shape, f32),
            pltpu.VMEM(weights_owned.shape, f32),
            pltpu.VMEM((blocks, rows, width), f32),
            pltpu.SemaphoreType.DMA((1 + slots,)),
            pltpu.SemaphoreType.DMA((slots, 2)),
            pltpu.SemaphoreType.DMA(()),
        ],
        compiler_params=params(basis, weights_owned, weights_owned, weights_owned, replica_delta),
        name="final",
    )(
        stay(owner_of), stay(layer_of), partial, high, low, held, first,
        chosen, near_across, far, far_across, weights,
    )
    return (new_weights, new_momentum, replica_weights)


def solution(mesh):
    placed = (
        P("rep", None, "own", None),
        P(),
        P(),
        P(),
        P("own", None, None),
        P("own", None, None),
    )
    return jax.shard_map(
        local,
        mesh=mesh,
        in_specs=placed,
        out_specs=(P("own", None, None), P("own", None, None), P(None, "own", None)),
        check_vma=False,
    )
```

```python
import math

import jax
import jax.numpy as jnp
from jax import lax
from jax.experimental import pallas as pl
from jax.experimental.pallas import tpu as pltpu
from jax.sharding import PartitionSpec as P

momentum_decay = 0.9
outer_rate = 0.7
carried = outer_rate * momentum_decay * momentum_decay
total_rate = outer_rate * (1.0 + momentum_decay)

VMEM = pl.BlockSpec(memory_space=pltpu.VMEM)
SMEM = pl.BlockSpec(memory_space=pltpu.SMEM)
HBM = pl.BlockSpec(memory_space=pltpu.HBM)
ANY = pl.BlockSpec(memory_space=pl.ANY)


def params(*arrays):
    held = sum(4 * math.prod(array.shape) for array in arrays)
    return pltpu.CompilerParams(vmem_limit_bytes=2 * held + 4 * 1024 * 1024)


def position():
    rep = lax.axis_index("rep")
    return lax.rem(rep, 2), rep // 2


def split(array):
    high = array.astype(jnp.bfloat16)
    low = (array - high.astype(jnp.float32)).astype(jnp.bfloat16)
    return high, low


def product(left, right_high, right_low, contract=((1,), (0,))):
    rows = left.shape[0]
    high, low = split(left)

    def dot(a, b):
        return lax.dot_general(
            a, b, (contract, ((), ())), preferred_element_type=jnp.float32
        )

    both = dot(jnp.concatenate([high, low], axis=0), right_high)
    return both[:rows] + (both[rows:] + dot(high, right_low))


def place_of(owner_ref, block):
    owner = owner_ref[block]
    slot = jnp.int32(0)
    for earlier in range(block):
        slot = slot + jnp.where(owner_ref[earlier] == owner, 1, 0)
    return owner, slot


def outset_kernel(
    owner_ref, layer_ref, delta_ref, basis_ref, weights_ref, momentum_ref,
    sent_ref, coeffs_ref,
    owner_smem, layer_smem, delta_vmem, basis_vmem, w_ref, m_ref, made_ref, in_sems, out_sems,
):
    owners, rows, total = sent_ref.shape
    blocks, _, width = delta_ref.shape
    layers, rank, _ = basis_ref.shape
    columns = width // 2
    core, across = position()
    part = pl.ds(pl.multiple_of(core * columns, 128), columns)
    loads = [
        pltpu.make_async_copy(source, target, in_sems.at[index])
        for index, (source, target) in enumerate((
            (owner_ref, owner_smem),
            (layer_ref, layer_smem),
            (delta_ref, delta_vmem),
            *[(basis_ref.at[layer], basis_vmem.at[layer]) for layer in range(layers)],
            (weights_ref.at[:, :, part], w_ref),
            (momentum_ref.at[:, :, part], m_ref),
        ))
    ]
    for load in loads[:-2]:
        load.start()
    loads[2].wait()
    loads[-2].start()
    loads[-1].start()
    for load in loads[3:-2]:
        load.wait()
    high, low = split(basis_vmem[...].reshape(layers * rank, width))
    products = product(delta_vmem[...].reshape(blocks * rows, width), high, low, ((1,), (1,)))
    loads[-2].wait()
    loads[-1].wait()
    upper = lax.broadcasted_iota(jnp.int32, (rows, columns), 0) < rows // 2
    for owner in range(owners):
        here = pl.ds(owner * rows, rows)
        first, second = [
            w_ref[slot, here, :] - carried * m_ref[slot, here, :] for slot in range(2)
        ]
        for side in range(2):

            @pl.when(across == side)
            def _():
                if side == 0:
                    tile = jnp.where(upper, first, pltpu.roll(second, rows // 2, 0))
                else:
                    tile = jnp.where(upper, pltpu.roll(first, rows // 2, 0), second)
                made_ref[owner, :, :columns] = tile
    early = pltpu.make_async_copy(
        made_ref.at[:, :, :columns], sent_ref.at[:, :, :columns], out_sems.at[0]
    )
    early.start()
    loads[0].wait()
    loads[1].wait()
    lane = lax.broadcasted_iota(jnp.int32, (rows, 2 * rank), 1)
    coeffs_ref[...] = jnp.zeros_like(coeffs_ref)
    for block in range(blocks):
        owner, slot = place_of(owner_smem, block)
        folded = jnp.zeros((rows, 2 * rank), jnp.float32)
        for pair in range(layers // 2):
            own = products[block * rows:(block + 1) * rows, 2 * rank * pair:2 * rank * (pair + 1)]
            folded = folded + jnp.where(2 * pair + lane // rank == layer_smem[block], own, 0.0)
        folded = folded + pltpu.roll(folded, rank, 1)
        placed = jnp.where(lane // rank == slot, folded, 0.0)
        coeffs_ref[owner] = coeffs_ref[owner] + placed
    made_ref[:, :, columns:] = coeffs_ref[...]
    late = pltpu.make_async_copy(
        made_ref.at[:, :, columns:], sent_ref.at[:, :, columns:], out_sems.at[1]
    )
    late.start()
    early.wait()
    late.wait()


def held_by(me, slot, owner_ref, layer_ref):
    used, layer = jnp.int32(0), jnp.int32(0)
    for block in range(owner_ref.shape[0]):
        owner, place = place_of(owner_ref, block)
        here = (owner == me) & (place == slot)
        layer = jnp.where(here, layer_ref[block], layer)
        used = jnp.where(here, 1, used)
    return used, layer


def prepare_kernel(
    reps, owner_ref, layer_ref, coeffs_ref, basis_ref, momentum_ref, weights_ref,
    grad_ref, high_ref, low_ref, held_ref, first_ref, marks_ref,
    wide_ref, basis_vmem, slot_vmem, sems,
):
    pairs, rows, columns = grad_ref.shape
    blocks = owner_ref.shape[0]
    layers, rank, width = basis_ref.shape
    slots = momentum_ref.shape[0]
    places = coeffs_ref.shape[0] * slots
    me = lax.axis_index("own")
    core, across = position()
    part = pl.ds(pl.multiple_of(core * columns, 128), columns)
    found = [held_by(me, slot, owner_ref, layer_ref) for slot in range(slots)]
    loads = [pltpu.make_async_copy(basis_ref.at[:, :, part], basis_vmem, sems.at[0])]
    for slot in range(slots):
        loads.append(
            pltpu.make_async_copy(basis_ref.at[found[slot][1]], slot_vmem.at[slot], sems.at[1 + slot])
        )
    loads.append(pltpu.make_async_copy(momentum_ref, held_ref, sems.at[1 + slots]))
    loads.append(pltpu.make_async_copy(weights_ref.at[0], first_ref, sems.at[2 + slots]))
    for load in loads:
        load.start()
    lane = lax.broadcasted_iota(jnp.int32, (rows, 2 * rank), 1)
    wide_lane = lax.broadcasted_iota(jnp.int32, (rows, layers * rank), 1)
    place_row = lax.broadcasted_iota(jnp.int32, (places, marks_ref.shape[1]), 0)
    upper = lax.broadcasted_iota(jnp.int32, (rows, layers * rank), 0) < rows // 2
    for pair in range(pairs):
        parts = []
        for odd in range(2):
            block = 2 * pair + odd
            owner, slot = place_of(owner_ref, block)
            both = jnp.where(lane // rank == slot, coeffs_ref[owner], 0.0)
            both = both + pltpu.roll(both, rank, 1)
            wide = jnp.concatenate([both] * (layers // 2), axis=1)
            wide = jnp.where(wide_lane // rank == layer_ref[block], wide, 0.0)
            parts.append(jnp.where(across == odd, wide, pltpu.roll(wide, rows // 2, 0)))
            marks_ref[pl.ds(block * places, places), :] = jnp.where(
                place_row == owner * slots + slot, 1.0, 0.0
            )
        wide_ref[pl.ds(pair * rows, rows), :] = jnp.where(upper, parts[0], parts[1])
    loads[0].wait()
    high, low = split(basis_vmem[...].reshape(layers * rank, columns))
    grad = product(wide_ref[...] * (total_rate / reps), high, low)
    grad_ref[...] = grad.reshape(pairs, rows, columns)
    for slot in range(slots):
        loads[1 + slot].wait()
        slot_high, slot_low = split(slot_vmem[slot])
        high_ref[slot] = slot_high
        low_ref[slot] = slot_low
    loads[-2].wait()
    loads[-1].wait()
    for slot in range(slots):

        @pl.when(found[slot][0] == 0)
        def _():
            high_ref[slot] = jnp.zeros_like(high_ref[slot])
            low_ref[slot] = jnp.zeros_like(low_ref[slot])
            held_ref[slot] = jnp.zeros_like(held_ref[slot])
            if slot == 0:
                first_ref[...] = jnp.zeros_like(first_ref)


def select_kernel(near_ref, grad_ref, marks_ref, chosen_ref):
    pairs, rows, columns = chosen_ref.shape
    owners = near_ref.shape[0]
    lanes = marks_ref.shape[1]
    upper = lax.broadcasted_iota(jnp.int32, (rows, columns), 0) < rows // 2

    def one(pair, carry):
        parts = []
        for odd in range(2):
            first = (2 * pair + odd) * 2 * owners
            sums = []
            for slot in range(2):
                total = jnp.zeros((rows, columns), jnp.float32)
                for owner in range(owners):
                    mark = marks_ref[pl.ds(first + 2 * owner + slot, 1), :]
                    mark = jnp.concatenate([mark] * (columns // lanes), axis=1)
                    total = total + mark * near_ref[owner, :, :columns]
                sums.append(total)
            parts.append(sums[odd] + pltpu.roll(sums[1 - odd], rows // 2, 0))
        chosen_ref[pair] = jnp.where(upper, parts[0], parts[1]) - grad_ref[pair]
        return carry

    lax.fori_loop(0, pairs, one, 0, unroll=pairs <= 4)


def after_kernel(rows_ref, done_ref, same_ref):
    pass


def final_kernel(
    reps, owner_ref, layer_ref, coeffs_ref, high_ref, low_ref, momentum_ref, first_ref,
    near_ref, near_across_ref, far_ref, far_across_ref, weights_ref,
    new_weights_ref, new_momentum_ref, replica_ref,
    owner_smem, layer_smem, w_ref, m_ref, change_ref, rows_ref, in_sems, out_sems, rows_sem,
):
    slots, rows, width = weights_ref.shape
    rank = high_ref.shape[1]
    pairs, tile, columns = near_ref.shape
    me = lax.axis_index("own")
    core, across = position()
    sources = [(owner_ref, owner_smem), (layer_ref, layer_smem)]
    sources += [(weights_ref.at[slot], w_ref.at[slot]) for slot in range(1, slots)]
    loads = [
        pltpu.make_async_copy(source, target, in_sems.at[index])
        for index, (source, target) in enumerate(sources)
    ]
    for load in loads:
        load.start()
    stores = []
    averaged = coeffs_ref[...].reshape(rows, slots * rank) * (1.0 / reps)

    def send(source, target, slot, which):
        store = pltpu.make_async_copy(source.at[slot], target.at[slot], out_sems.at[slot, which])
        store.start()
        stores.append(store)

    for slot in range(slots):
        grad = product(
            averaged[:, slot * rank:(slot + 1) * rank], high_ref[slot], low_ref[slot]
        )
        momentum = momentum_decay * momentum_ref[slot] + grad
        m_ref[slot] = momentum
        send(m_ref, new_momentum_ref, slot, 0)
        change = outer_rate * (grad + momentum_decay * momentum)
        if slot == 0:
            w_ref[0] = first_ref[...] - change
            send(w_ref, new_weights_ref, 0, 1)
        else:
            change_ref[slot] = change
    upper = lax.broadcasted_iota(jnp.int32, (tile, columns), 0) < tile // 2
    for near_core in range(2):
        for near_across in range(2):

            @pl.when((core == near_core) & (across == near_across))
            def _():
                for side, sources in (
                    (near_core, (near_ref, near_across_ref)),
                    (1 - near_core, (far_ref, far_across_ref)),
                ):
                    top, bottom = sources if near_across == 0 else sources[::-1]
                    here = pl.ds(side * columns, columns)
                    for pair in range(pairs):
                        above, below = top[pair], bottom[pair]
                        rows_ref[2 * pair, :, here] = jnp.where(
                            upper, above, pltpu.roll(below, tile // 2, 0)
                        )
                        rows_ref[2 * pair + 1, :, here] = jnp.where(
                            upper, pltpu.roll(above, tile // 2, 0), below
                        )

    store = pltpu.make_async_copy(rows_ref, replica_ref, rows_sem)
    store.start()
    stores.append(store)
    for load in loads[:2]:
        load.wait()
    for slot in range(1, slots):
        used, _ = held_by(me, slot, owner_smem, layer_smem)
        loads[1 + slot].wait()
        w_ref[slot] = jnp.where(used == 1, w_ref[slot] - change_ref[slot], 0.0)
        send(w_ref, new_weights_ref, slot, 1)
    for store in stores:
        store.wait()


def local(replica_delta, layer_basis, layer_of, owner_of, weights_owned, momentum_owned):
    own_count = lax.axis_size("own")
    rep_count = lax.axis_size("rep")
    slots, owned_rows, width = weights_owned.shape
    blocks, rows = replica_delta.shape[1:3]
    layers, _, rank = layer_basis.shape
    f32, bf16 = jnp.float32, jnp.bfloat16
    shape = jax.ShapeDtypeStruct
    columns = width // 2
    total = columns + slots * rank
    basis = jnp.swapaxes(layer_basis, 1, 2)

    def stay(array):
        return pltpu.with_memory_space_constraint(array, pltpu.HBM)

    weights, momentum = stay(weights_owned), stay(momentum_owned)

    def swap(array, bits):
        pairs = [(rep, rep ^ bits) for rep in range(rep_count)]
        return lax.ppermute(array, "rep", pairs)

    sent, coeffs = pl.pallas_call(
        outset_kernel,
        out_shape=[
            shape((own_count, rows, total), f32),
            shape((own_count, rows, slots * rank), f32),
        ],
        in_specs=[HBM] * 6,
        out_specs=[HBM, VMEM],
        scratch_shapes=[
            pltpu.SMEM(owner_of.shape, jnp.int32),
            pltpu.SMEM(layer_of.shape, jnp.int32),
            pltpu.VMEM(replica_delta.shape[1:], f32),
            pltpu.VMEM(basis.shape, f32),
            pltpu.VMEM((slots, owned_rows, columns), f32),
            pltpu.VMEM((slots, owned_rows, columns), f32),
            pltpu.VMEM((own_count, rows, total), f32),
            pltpu.SemaphoreType.DMA((5 + layers,)),
            pltpu.SemaphoreType.DMA((2,)),
        ],
        compiler_params=params(replica_delta, basis, basis, weights_owned),
        name="outset",
    )(stay(owner_of), stay(layer_of), stay(replica_delta[0]), stay(basis), weights, momentum)
    near = lax.all_to_all(sent, "own", split_axis=0, concat_axis=0, tiled=True)

    coeffs = coeffs + swap(coeffs, 1)
    coeffs = coeffs + swap(coeffs, 2)
    grad, high, low, held, first, marks = pl.pallas_call(
        lambda *refs: prepare_kernel(rep_count, *refs),
        out_shape=[
            shape((blocks // 2, rows, columns), f32),
            shape((slots, rank, width), bf16),
            shape((slots, rank, width), bf16),
            shape(momentum_owned.shape, f32),
            shape(weights_owned.shape[1:], f32),
            shape((blocks * own_count * slots, 128), f32),
        ],
        in_specs=[SMEM, SMEM, VMEM, HBM, HBM, HBM],
        out_specs=[VMEM] * 6,
        scratch_shapes=[
            pltpu.VMEM((blocks // 2 * rows, layers * rank), f32),
            pltpu.VMEM((layers, rank, columns), f32),
            pltpu.VMEM((slots, rank, width), f32),
            pltpu.SemaphoreType.DMA((3 + slots,)),
        ],
        compiler_params=params(basis, replica_delta, replica_delta, momentum_owned, momentum_owned),
        name="prepare",
    )(owner_of, layer_of, coeffs, stay(basis), momentum, weights)

    def after(array, done):
        return pl.pallas_call(
            after_kernel,
            out_shape=shape(array.shape, f32),
            in_specs=[ANY, ANY],
            out_specs=ANY,
            input_output_aliases={0: 0},
            compiler_params=params(),
            name="after",
        )(array, done)

    near = after(near, grad)
    partial = near[:, :, columns:]
    partial = (partial + swap(partial, 1)) + (swap(partial, 2) + swap(partial, 3))
    chosen = pl.pallas_call(
        select_kernel,
        out_shape=shape((blocks // 2, rows, columns), f32),
        in_specs=[VMEM] * 3,
        out_specs=VMEM,
        compiler_params=params(near, near, marks),
        name="select",
    )(near, grad, marks)
    far = swap(chosen, 1)
    near_across = swap(chosen, 2)
    far_across = swap(near_across, 1)
    new_weights, new_momentum, replica_weights = pl.pallas_call(
        lambda *refs: final_kernel(rep_count, *refs),
        out_shape=[
            shape(weights_owned.shape, f32),
            shape(weights_owned.shape, f32),
            shape((blocks, rows, width), f32),
        ],
        in_specs=[HBM, HBM] + [VMEM] * 9 + [HBM],
        out_specs=[HBM] * 3,
        scratch_shapes=[
            pltpu.SMEM(owner_of.shape, jnp.int32),
            pltpu.SMEM(layer_of.shape, jnp.int32),
            pltpu.VMEM(weights_owned.shape, f32),
            pltpu.VMEM(weights_owned.shape, f32),
            pltpu.VMEM(weights_owned.shape, f32),
            pltpu.VMEM((blocks, rows, width), f32),
            pltpu.SemaphoreType.DMA((1 + slots,)),
            pltpu.SemaphoreType.DMA((slots, 2)),
            pltpu.SemaphoreType.DMA(()),
        ],
        compiler_params=params(basis, weights_owned, weights_owned, weights_owned, replica_delta),
        name="final",
    )(
        stay(owner_of), stay(layer_of), partial, high, low, held, first,
        chosen, near_across, far, far_across, weights,
    )
    return (new_weights, new_momentum, replica_weights)


def solution(mesh):
    placed = (
        P("rep", None, "own", None),
        P(),
        P(),
        P(),
        P("own", None, None),
        P("own", None, None),
    )
    return jax.shard_map(
        local,
        mesh=mesh,
        in_specs=placed,
        out_specs=(P("own", None, None), P("own", None, None), P(None, "own", None)),
        check_vma=False,
    )
```

```python
import math

import jax
import jax.numpy as jnp
from jax import lax
from jax.experimental import pallas as pl
from jax.experimental.pallas import tpu as pltpu
from jax.sharding import PartitionSpec as P

momentum_decay = 0.9
outer_rate = 0.7
carried = outer_rate * momentum_decay * momentum_decay
total_rate = outer_rate * (1.0 + momentum_decay)

VMEM = pl.BlockSpec(memory_space=pltpu.VMEM)
SMEM = pl.BlockSpec(memory_space=pltpu.SMEM)
HBM = pl.BlockSpec(memory_space=pltpu.HBM)
ANY = pl.BlockSpec(memory_space=pl.ANY)


def params(*arrays):
    held = sum(4 * math.prod(array.shape) for array in arrays)
    return pltpu.CompilerParams(vmem_limit_bytes=2 * held + 4 * 1024 * 1024)


def position():
    rep = lax.axis_index("rep")
    return lax.rem(rep, 2), rep // 2


def split(array):
    high = array.astype(jnp.bfloat16)
    low = (array - high.astype(jnp.float32)).astype(jnp.bfloat16)
    return high, low


def product(left, right_high, right_low, contract=((1,), (0,))):
    rows = left.shape[0]
    high, low = split(left)

    def dot(a, b):
        return lax.dot_general(
            a, b, (contract, ((), ())), preferred_element_type=jnp.float32
        )

    both = dot(jnp.concatenate([high, low], axis=0), right_high)
    return both[:rows] + (both[rows:] + dot(high, right_low))


def place_of(owner_ref, block):
    owner = owner_ref[block]
    slot = jnp.int32(0)
    for earlier in range(block):
        slot = slot + jnp.where(owner_ref[earlier] == owner, 1, 0)
    return owner, slot


def outset_kernel(
    owner_ref, layer_ref, delta_ref, basis_ref, weights_ref, momentum_ref,
    sent_ref, coeffs_ref,
    owner_smem, layer_smem, delta_vmem, basis_vmem, w_ref, m_ref, made_ref, in_sems, out_sems,
):
    owners, rows, total = sent_ref.shape
    blocks, _, width = delta_ref.shape
    layers, rank, _ = basis_ref.shape
    columns = width // 2
    core, across = position()
    part = pl.ds(pl.multiple_of(core * columns, 128), columns)
    loads = [
        pltpu.make_async_copy(source, target, in_sems.at[index])
        for index, (source, target) in enumerate((
            (delta_ref, delta_vmem),
            *[(basis_ref.at[layer], basis_vmem.at[layer]) for layer in range(layers)],
            (weights_ref.at[:, :, part], w_ref),
            (momentum_ref.at[:, :, part], m_ref),
            (owner_ref, owner_smem),
            (layer_ref, layer_smem),
        ))
    ]
    for load in loads:
        load.start()
    for load in loads[:1 + layers]:
        load.wait()
    high, low = split(basis_vmem[...].reshape(layers * rank, width))
    products = product(delta_vmem[...].reshape(blocks * rows, width), high, low, ((1,), (1,)))
    for load in loads[1 + layers:]:
        load.wait()
    upper = lax.broadcasted_iota(jnp.int32, (rows, columns), 0) < rows // 2
    for owner in range(owners):
        here = pl.ds(owner * rows, rows)
        first, second = [
            w_ref[slot, here, :] - carried * m_ref[slot, here, :] for slot in range(2)
        ]
        made_ref[owner, :, :columns] = jnp.where(
            across == 0,
            jnp.where(upper, first, pltpu.roll(second, rows // 2, 0)),
            jnp.where(upper, pltpu.roll(first, rows // 2, 0), second),
        )
    early = pltpu.make_async_copy(
        made_ref.at[:, :, :columns], sent_ref.at[:, :, :columns], out_sems.at[0]
    )
    early.start()
    lane = lax.broadcasted_iota(jnp.int32, (rows, 2 * rank), 1)
    coeffs_ref[...] = jnp.zeros_like(coeffs_ref)
    for block in range(blocks):
        owner, slot = place_of(owner_smem, block)
        folded = jnp.zeros((rows, 2 * rank), jnp.float32)
        for pair in range(layers // 2):
            own = products[block * rows:(block + 1) * rows, 2 * rank * pair:2 * rank * (pair + 1)]
            folded = folded + jnp.where(2 * pair + lane // rank == layer_smem[block], own, 0.0)
        folded = folded + pltpu.roll(folded, rank, 1)
        pltpu.store(coeffs_ref.at[owner], folded, mask=lane // rank == slot)
    made_ref[:, :, columns:] = coeffs_ref[...]
    late = pltpu.make_async_copy(
        made_ref.at[:, :, columns:], sent_ref.at[:, :, columns:], out_sems.at[1]
    )
    late.start()
    early.wait()
    late.wait()


def held_by(me, slot, owner_ref, layer_ref):
    used, layer = jnp.int32(0), jnp.int32(0)
    for block in range(owner_ref.shape[0]):
        owner, place = place_of(owner_ref, block)
        here = (owner == me) & (place == slot)
        layer = jnp.where(here, layer_ref[block], layer)
        used = jnp.where(here, 1, used)
    return used, layer


def prepare_kernel(
    reps, owner_ref, layer_ref, coeffs_ref, basis_ref, momentum_ref, weights_ref,
    grad_ref, high_ref, low_ref, held_ref, first_ref, marks_ref,
    wide_ref, basis_vmem, slot_vmem, sems,
):
    pairs, rows, columns = grad_ref.shape
    blocks = owner_ref.shape[0]
    layers, rank, width = basis_ref.shape
    slots = momentum_ref.shape[0]
    places = coeffs_ref.shape[0] * slots
    me = lax.axis_index("own")
    core, across = position()
    part = pl.ds(pl.multiple_of(core * columns, 128), columns)
    found = [held_by(me, slot, owner_ref, layer_ref) for slot in range(slots)]
    loads = [pltpu.make_async_copy(basis_ref.at[:, :, part], basis_vmem, sems.at[0])]
    for slot in range(slots):
        loads.append(
            pltpu.make_async_copy(basis_ref.at[found[slot][1]], slot_vmem.at[slot], sems.at[1 + slot])
        )
    loads.append(pltpu.make_async_copy(momentum_ref, held_ref, sems.at[1 + slots]))
    loads.append(pltpu.make_async_copy(weights_ref.at[0], first_ref, sems.at[2 + slots]))
    for load in loads:
        load.start()
    lane = lax.broadcasted_iota(jnp.int32, (rows, 2 * rank), 1)
    wide_lane = lax.broadcasted_iota(jnp.int32, (rows, layers * rank), 1)
    place_row = lax.broadcasted_iota(jnp.int32, (places, marks_ref.shape[1]), 0)
    upper = lax.broadcasted_iota(jnp.int32, (rows, layers * rank), 0) < rows // 2
    for pair in range(pairs):
        parts = []
        for odd in range(2):
            block = 2 * pair + odd
            owner, slot = place_of(owner_ref, block)
            both = jnp.where(lane // rank == slot, coeffs_ref[owner], 0.0)
            both = both + pltpu.roll(both, rank, 1)
            wide = jnp.concatenate([both] * (layers // 2), axis=1)
            wide = jnp.where(wide_lane // rank == layer_ref[block], wide, 0.0)
            parts.append(jnp.where(across == odd, wide, pltpu.roll(wide, rows // 2, 0)))
            marks_ref[pl.ds(block * places, places), :] = jnp.where(
                place_row == owner * slots + slot, 1.0, 0.0
            )
        wide_ref[pl.ds(pair * rows, rows), :] = jnp.where(upper, parts[0], parts[1])
    loads[0].wait()
    high, low = split(basis_vmem[...].reshape(layers * rank, columns))
    grad = product(wide_ref[...] * (total_rate / reps), high, low)
    grad_ref[...] = grad.reshape(pairs, rows, columns)
    for slot in range(slots):
        loads[1 + slot].wait()
        slot_high, slot_low = split(slot_vmem[slot])
        high_ref[slot] = slot_high
        low_ref[slot] = slot_low
    loads[-2].wait()
    loads[-1].wait()
    for slot in range(slots):

        @pl.when(found[slot][0] == 0)
        def _():
            high_ref[slot] = jnp.zeros_like(high_ref[slot])
            low_ref[slot] = jnp.zeros_like(low_ref[slot])
            held_ref[slot] = jnp.zeros_like(held_ref[slot])
            if slot == 0:
                first_ref[...] = jnp.zeros_like(first_ref)


def select_kernel(near_ref, grad_ref, marks_ref, chosen_ref):
    pairs, rows, columns = chosen_ref.shape
    owners = near_ref.shape[0]
    lanes = marks_ref.shape[1]
    upper = lax.broadcasted_iota(jnp.int32, (rows, columns), 0) < rows // 2

    def one(pair, carry):
        parts = []
        for odd in range(2):
            first = (2 * pair + odd) * 2 * owners
            sums = []
            for slot in range(2):
                total = jnp.zeros((rows, columns), jnp.float32)
                for owner in range(owners):
                    mark = marks_ref[pl.ds(first + 2 * owner + slot, 1), :]
                    mark = jnp.concatenate([mark] * (columns // lanes), axis=1)
                    total = total + mark * near_ref[owner, :, :columns]
                sums.append(total)
            parts.append(sums[odd] + pltpu.roll(sums[1 - odd], rows // 2, 0))
        chosen_ref[pair] = jnp.where(upper, parts[0], parts[1]) - grad_ref[pair]
        return carry

    lax.fori_loop(0, pairs, one, 0, unroll=pairs <= 4)


def after_kernel(rows_ref, done_ref, same_ref):
    pass


def final_kernel(
    reps, owner_ref, layer_ref, coeffs_ref, high_ref, low_ref, momentum_ref, first_ref,
    near_ref, near_across_ref, far_ref, far_across_ref, weights_ref,
    new_weights_ref, new_momentum_ref, replica_ref,
    owner_smem, layer_smem, w_ref, m_ref, change_ref, rows_ref, in_sems, out_sems, rows_sem,
):
    slots, rows, width = weights_ref.shape
    rank = high_ref.shape[1]
    pairs, tile, columns = near_ref.shape
    me = lax.axis_index("own")
    core, across = position()
    sources = [(owner_ref, owner_smem), (layer_ref, layer_smem)]
    sources += [(weights_ref.at[slot], w_ref.at[slot]) for slot in range(1, slots)]
    loads = [
        pltpu.make_async_copy(source, target, in_sems.at[index])
        for index, (source, target) in enumerate(sources)
    ]
    for load in loads:
        load.start()
    stores = []
    averaged = coeffs_ref[...].reshape(rows, slots * rank) * (1.0 / reps)

    def send(source, target, slot, which):
        store = pltpu.make_async_copy(source.at[slot], target.at[slot], out_sems.at[slot, which])
        store.start()
        stores.append(store)

    for slot in range(slots):
        grad = product(
            averaged[:, slot * rank:(slot + 1) * rank], high_ref[slot], low_ref[slot]
        )
        momentum = momentum_decay * momentum_ref[slot] + grad
        m_ref[slot] = momentum
        send(m_ref, new_momentum_ref, slot, 0)
        change = outer_rate * (grad + momentum_decay * momentum)
        if slot == 0:
            w_ref[0] = first_ref[...] - change
            send(w_ref, new_weights_ref, 0, 1)
        else:
            change_ref[slot] = change
    upper = lax.broadcasted_iota(jnp.int32, (tile, columns), 0) < tile // 2
    for near_core in range(2):
        for near_across in range(2):

            @pl.when((core == near_core) & (across == near_across))
            def _():
                for side, sources in (
                    (near_core, (near_ref, near_across_ref)),
                    (1 - near_core, (far_ref, far_across_ref)),
                ):
                    top, bottom = sources if near_across == 0 else sources[::-1]
                    here = pl.ds(side * columns, columns)
                    for pair in range(pairs):
                        above, below = top[pair], bottom[pair]
                        rows_ref[2 * pair, :, here] = jnp.where(
                            upper, above, pltpu.roll(below, tile // 2, 0)
                        )
                        rows_ref[2 * pair + 1, :, here] = jnp.where(
                            upper, pltpu.roll(above, tile // 2, 0), below
                        )

    store = pltpu.make_async_copy(rows_ref, replica_ref, rows_sem)
    store.start()
    stores.append(store)
    for load in loads[:2]:
        load.wait()
    for slot in range(1, slots):
        used, _ = held_by(me, slot, owner_smem, layer_smem)
        loads[1 + slot].wait()
        w_ref[slot] = jnp.where(used == 1, w_ref[slot] - change_ref[slot], 0.0)
        send(w_ref, new_weights_ref, slot, 1)
    for store in stores:
        store.wait()


def local(replica_delta, layer_basis, layer_of, owner_of, weights_owned, momentum_owned):
    own_count = lax.axis_size("own")
    rep_count = lax.axis_size("rep")
    slots, owned_rows, width = weights_owned.shape
    blocks, rows = replica_delta.shape[1:3]
    layers, _, rank = layer_basis.shape
    f32, bf16 = jnp.float32, jnp.bfloat16
    shape = jax.ShapeDtypeStruct
    columns = width // 2
    total = columns + slots * rank
    basis = jnp.swapaxes(layer_basis, 1, 2)

    def stay(array):
        return pltpu.with_memory_space_constraint(array, pltpu.HBM)

    weights, momentum = stay(weights_owned), stay(momentum_owned)

    def swap(array, bits):
        pairs = [(rep, rep ^ bits) for rep in range(rep_count)]
        return lax.ppermute(array, "rep", pairs)

    sent, coeffs = pl.pallas_call(
        outset_kernel,
        out_shape=[
            shape((own_count, rows, total), f32),
            shape((own_count, rows, slots * rank), f32),
        ],
        in_specs=[HBM] * 6,
        out_specs=[HBM, VMEM],
        scratch_shapes=[
            pltpu.SMEM(owner_of.shape, jnp.int32),
            pltpu.SMEM(layer_of.shape, jnp.int32),
            pltpu.VMEM(replica_delta.shape[1:], f32),
            pltpu.VMEM(basis.shape, f32),
            pltpu.VMEM((slots, owned_rows, columns), f32),
            pltpu.VMEM((slots, owned_rows, columns), f32),
            pltpu.VMEM((own_count, rows, total), f32),
            pltpu.SemaphoreType.DMA((5 + layers,)),
            pltpu.SemaphoreType.DMA((2,)),
        ],
        compiler_params=params(replica_delta, basis, basis, weights_owned),
        name="outset",
    )(stay(owner_of), stay(layer_of), stay(replica_delta[0]), stay(basis), weights, momentum)
    near = lax.all_to_all(sent, "own", split_axis=0, concat_axis=0, tiled=True)

    coeffs = coeffs + swap(coeffs, 1)
    coeffs = coeffs + swap(coeffs, 2)
    grad, high, low, held, first, marks = pl.pallas_call(
        lambda *refs: prepare_kernel(rep_count, *refs),
        out_shape=[
            shape((blocks // 2, rows, columns), f32),
            shape((slots, rank, width), bf16),
            shape((slots, rank, width), bf16),
            shape(momentum_owned.shape, f32),
            shape(weights_owned.shape[1:], f32),
            shape((blocks * own_count * slots, 128), f32),
        ],
        in_specs=[SMEM, SMEM, VMEM, HBM, HBM, HBM],
        out_specs=[VMEM] * 6,
        scratch_shapes=[
            pltpu.VMEM((blocks // 2 * rows, layers * rank), f32),
            pltpu.VMEM((layers, rank, columns), f32),
            pltpu.VMEM((slots, rank, width), f32),
            pltpu.SemaphoreType.DMA((3 + slots,)),
        ],
        compiler_params=params(basis, replica_delta, replica_delta, momentum_owned, momentum_owned),
        name="prepare",
    )(owner_of, layer_of, coeffs, stay(basis), momentum, weights)

    def after(array, done):
        return pl.pallas_call(
            after_kernel,
            out_shape=shape(array.shape, f32),
            in_specs=[ANY, ANY],
            out_specs=ANY,
            input_output_aliases={0: 0},
            compiler_params=params(),
            name="after",
        )(array, done)

    near = after(near, grad)
    partial = near[:, :, columns:]
    partial = (partial + swap(partial, 1)) + (swap(partial, 2) + swap(partial, 3))
    chosen = pl.pallas_call(
        select_kernel,
        out_shape=shape((blocks // 2, rows, columns), f32),
        in_specs=[VMEM] * 3,
        out_specs=VMEM,
        compiler_params=params(near, near, marks),
        name="select",
    )(near, grad, marks)
    far = swap(chosen, 1)
    near_across = swap(chosen, 2)
    far_across = swap(near_across, 1)
    new_weights, new_momentum, replica_weights = pl.pallas_call(
        lambda *refs: final_kernel(rep_count, *refs),
        out_shape=[
            shape(weights_owned.shape, f32),
            shape(weights_owned.shape, f32),
            shape((blocks, rows, width), f32),
        ],
        in_specs=[HBM, HBM] + [VMEM] * 9 + [HBM],
        out_specs=[HBM] * 3,
        scratch_shapes=[
            pltpu.SMEM(owner_of.shape, jnp.int32),
            pltpu.SMEM(layer_of.shape, jnp.int32),
            pltpu.VMEM(weights_owned.shape, f32),
            pltpu.VMEM(weights_owned.shape, f32),
            pltpu.VMEM(weights_owned.shape, f32),
            pltpu.VMEM((blocks, rows, width), f32),
            pltpu.SemaphoreType.DMA((1 + slots,)),
            pltpu.SemaphoreType.DMA((slots, 2)),
            pltpu.SemaphoreType.DMA(()),
        ],
        compiler_params=params(basis, weights_owned, weights_owned, weights_owned, replica_delta),
        name="final",
    )(
        stay(owner_of), stay(layer_of), partial, high, low, held, first,
        chosen, near_across, far, far_across, weights,
    )
    return (new_weights, new_momentum, replica_weights)


def solution(mesh):
    placed = (
        P("rep", None, "own", None),
        P(),
        P(),
        P(),
        P("own", None, None),
        P("own", None, None),
    )
    return jax.shard_map(
        local,
        mesh=mesh,
        in_specs=placed,
        out_specs=(P("own", None, None), P("own", None, None), P(None, "own", None)),
        check_vma=False,
    )
```

```python
import functools
import math

import jax
import jax.numpy as jnp
from jax import lax
from jax.experimental import pallas as pl
from jax.experimental.pallas import tpu as pltpu
from jax.sharding import PartitionSpec as P

momentum_decay = 0.9
outer_rate = 0.7
carried = outer_rate * momentum_decay * momentum_decay
total_rate = outer_rate * (1.0 + momentum_decay)

VMEM = pl.BlockSpec(memory_space=pltpu.VMEM)
SMEM = pl.BlockSpec(memory_space=pltpu.SMEM)
HBM = pl.BlockSpec(memory_space=pltpu.HBM)
ANY = pl.BlockSpec(memory_space=pl.ANY)


def params(*arrays):
    held = sum(4 * math.prod(array.shape) for array in arrays)
    return pltpu.CompilerParams(vmem_limit_bytes=2 * held + 4 * 1024 * 1024)


def position():
    rep = lax.axis_index("rep")
    return lax.rem(rep, 2), rep // 2


def split(array):
    high = array.astype(jnp.bfloat16)
    low = (array - high.astype(jnp.float32)).astype(jnp.bfloat16)
    return high, low


def product(left, right_high, right_low, contract=((1,), (0,))):
    rows = left.shape[0]
    high, low = split(left)

    def dot(a, b):
        return lax.dot_general(
            a, b, (contract, ((), ())), preferred_element_type=jnp.float32
        )

    both = dot(jnp.concatenate([high, low], axis=0), right_high)
    return both[:rows] + (both[rows:] + dot(high, right_low))


def place_of(owner_ref, block):
    owner = owner_ref[block]
    slot = jnp.int32(0)
    for earlier in range(block):
        slot = slot + jnp.where(owner_ref[earlier] == owner, 1, 0)
    return owner, slot


def shared(places, block):
    owner, _ = places[block]
    held, before = jnp.int32(0), jnp.int32(0)
    for other_owner, other_slot in places:
        held = held + jnp.where(other_owner == owner, 1, 0)
        before = before + jnp.where((other_slot == 1) & (other_owner < owner), 1, 0)
    return held == 2, before


def outset_kernel(
    owner_ref, layer_ref, delta_ref, basis_ref, weights_ref, momentum_ref,
    sent_ref, coeffs_ref,
    owner_smem, layer_smem, delta_vmem, basis_vmem, w_ref, m_ref, made_ref, in_sems, out_sems,
):
    owners, rows, total = sent_ref.shape
    blocks, _, width = delta_ref.shape
    layers, rank, _ = basis_ref.shape
    columns = width // 2
    core, across = position()
    part = pl.ds(pl.multiple_of(core * columns, 128), columns)
    loads = [
        pltpu.make_async_copy(source, target, in_sems.at[index])
        for index, (source, target) in enumerate((
            (delta_ref, delta_vmem),
            *[(basis_ref.at[layer], basis_vmem.at[layer]) for layer in range(layers)],
            (weights_ref.at[:, :, part], w_ref),
            (momentum_ref.at[:, :, part], m_ref),
            (owner_ref, owner_smem),
            (layer_ref, layer_smem),
        ))
    ]
    for load in loads:
        load.start()
    for load in loads[:1 + layers]:
        load.wait()
    high, low = split(basis_vmem[...].reshape(layers * rank, width))
    products = product(delta_vmem[...].reshape(blocks * rows, width), high, low, ((1,), (1,)))
    for load in loads[1 + layers:]:
        load.wait()
    upper = lax.broadcasted_iota(jnp.int32, (rows, columns), 0) < rows // 2
    me = lax.axis_index("own")
    held = jnp.int32(0)
    for block in range(blocks):
        held = held + jnp.where(owner_smem[block] == me, 1, 0)
    for owner in range(owners):
        here = pl.ds(owner * rows, rows)
        first, second = [
            w_ref[slot, here, :] - carried * m_ref[slot, here, :] for slot in range(2)
        ]
        halves = jnp.where(
            across == 0,
            jnp.where(upper, first, pltpu.roll(second, rows // 2, 0)),
            jnp.where(upper, pltpu.roll(first, rows // 2, 0), second),
        )
        made_ref[owner, :, :columns] = jnp.where(held == 2, halves, first)
    early = pltpu.make_async_copy(
        made_ref.at[:, :, :columns], sent_ref.at[:, :, :columns], out_sems.at[0]
    )
    early.start()
    lane = lax.broadcasted_iota(jnp.int32, (rows, 2 * rank), 1)
    coeffs_ref[...] = jnp.zeros_like(coeffs_ref)
    for block in range(blocks):
        owner, slot = place_of(owner_smem, block)
        folded = jnp.zeros((rows, 2 * rank), jnp.float32)
        for pair in range(layers // 2):
            own = products[block * rows:(block + 1) * rows, 2 * rank * pair:2 * rank * (pair + 1)]
            folded = folded + jnp.where(2 * pair + lane // rank == layer_smem[block], own, 0.0)
        folded = folded + pltpu.roll(folded, rank, 1)
        pltpu.store(coeffs_ref.at[owner], folded, mask=lane // rank == slot)
    made_ref[:, :, columns:] = coeffs_ref[...]
    late = pltpu.make_async_copy(
        made_ref.at[:, :, columns:], sent_ref.at[:, :, columns:], out_sems.at[1]
    )
    late.start()
    early.wait()
    late.wait()


def held_by(me, slot, owner_ref, layer_ref):
    used, layer = jnp.int32(0), jnp.int32(0)
    for block in range(owner_ref.shape[0]):
        owner, place = place_of(owner_ref, block)
        here = (owner == me) & (place == slot)
        layer = jnp.where(here, layer_ref[block], layer)
        used = jnp.where(here, 1, used)
    return used, layer


def prepare_kernel(
    reps, owner_ref, layer_ref, coeffs_ref, basis_ref, momentum_ref, weights_ref,
    grad_ref, high_ref, low_ref, held_ref, first_ref, marks_ref, codes_ref,
    wide_ref, basis_vmem, slot_vmem, sems,
):
    owners, rows, columns = grad_ref.shape
    blocks = owner_ref.shape[0]
    layers, rank, width = basis_ref.shape
    slots = momentum_ref.shape[0]
    me = lax.axis_index("own")
    core, across = position()
    part = pl.ds(pl.multiple_of(core * columns, 128), columns)
    found = [held_by(me, slot, owner_ref, layer_ref) for slot in range(slots)]
    loads = [pltpu.make_async_copy(basis_ref.at[:, :, part], basis_vmem, sems.at[0])]
    for slot in range(slots):
        loads.append(
            pltpu.make_async_copy(basis_ref.at[found[slot][1]], slot_vmem.at[slot], sems.at[1 + slot])
        )
    loads.append(pltpu.make_async_copy(momentum_ref, held_ref, sems.at[1 + slots]))
    loads.append(pltpu.make_async_copy(weights_ref.at[0], first_ref, sems.at[2 + slots]))
    for load in loads:
        load.start()
    lane = lax.broadcasted_iota(jnp.int32, (rows, 2 * rank), 1)
    wide_lane = lax.broadcasted_iota(jnp.int32, (rows, layers * rank), 1)
    half = lax.broadcasted_iota(jnp.int32, (rows, layers * rank), 0) // (rows // 2)
    wide_ref[...] = jnp.zeros_like(wide_ref)
    marks_ref[...] = jnp.zeros_like(marks_ref)
    places = [place_of(owner_ref, block) for block in range(blocks)]
    for block in range(blocks):
        owner, slot = places[block]
        two, before = shared(places, block)
        both = jnp.where(lane // rank == slot, coeffs_ref[owner], 0.0)
        both = both + pltpu.roll(both, rank, 1)
        wide = jnp.concatenate([both] * (layers // 2), axis=1)
        wide = jnp.where(wide_lane // rank == layer_ref[block], wide, 0.0)
        codes_ref[4 * block] = owner
        codes_ref[4 * block + 1] = slot
        codes_ref[4 * block + 2] = jnp.where(two, 1, 0)
        codes_ref[4 * block + 3] = jnp.where(two, before, 0)
        halves = jnp.where(slot == across, wide, pltpu.roll(wide, rows // 2, 0))
        halves = jnp.where(half == slot, halves, 0.0)
        wide_ref[owner] = wide_ref[owner] + jnp.where(two, halves, wide)

        @pl.when(slot == 1)
        def _():
            marks_ref[pl.ds(before * owners + owner, 1), :] = jnp.ones(
                (1, marks_ref.shape[1]), jnp.float32
            )

    loads[0].wait()
    high, low = split(basis_vmem[...].reshape(layers * rank, columns))
    wide = wide_ref[...].reshape(owners * rows, layers * rank)
    grad = product(wide * (total_rate / reps), high, low)
    grad_ref[...] = grad.reshape(owners, rows, columns)
    for slot in range(slots):
        loads[1 + slot].wait()
        slot_high, slot_low = split(slot_vmem[slot])
        high_ref[slot] = slot_high
        low_ref[slot] = slot_low
    loads[-2].wait()
    loads[-1].wait()
    for slot in range(slots):
        codes_ref[4 * blocks + slot] = found[slot][0]

        @pl.when(found[slot][0] == 0)
        def _():
            high_ref[slot] = jnp.zeros_like(high_ref[slot])
            low_ref[slot] = jnp.zeros_like(low_ref[slot])
            held_ref[slot] = jnp.zeros_like(held_ref[slot])
            if slot == 0:
                first_ref[...] = jnp.zeros_like(first_ref)


def select_kernel(near_ref, grad_ref, marks_ref, new_ref, given_ref):
    owners, rows, columns = new_ref.shape
    lanes = marks_ref.shape[1]
    for owner in range(owners):
        new_ref[owner] = near_ref[owner, :, :columns] - grad_ref[owner]

    def one(place, carry):
        total = jnp.zeros((rows, columns), jnp.float32)
        for owner in range(owners):
            mark = marks_ref[pl.ds(place * owners + owner, 1), :]
            mark = jnp.concatenate([mark] * (columns // lanes), axis=1)
            total = total + mark * new_ref[owner]
        given_ref[place] = total
        return carry

    lax.fori_loop(0, given_ref.shape[0], one, 0, unroll=given_ref.shape[0] <= 4)


def after_kernel(rows_ref, done_ref, same_ref):
    pass


def final_kernel(
    reps, codes_ref, coeffs_ref, high_ref, low_ref, momentum_ref, first_ref,
    near_ref, near_across_ref, far_ref, far_across_ref, weights_ref,
    new_weights_ref, new_momentum_ref, replica_ref,
    codes_smem, w_ref, m_ref, change_ref, rows_ref, in_sems, out_sems, rows_sem,
):
    slots, rows, width = weights_ref.shape
    rank = high_ref.shape[1]
    blocks = replica_ref.shape[0]
    _, tile, columns = near_ref.shape
    core, across = position()
    sources = [(weights_ref.at[slot], w_ref.at[slot]) for slot in range(1, slots)]
    sources.append((codes_ref, codes_smem))
    loads = [
        pltpu.make_async_copy(source, target, in_sems.at[index])
        for index, (source, target) in enumerate(sources)
    ]
    for load in loads:
        load.start()
    averaged = coeffs_ref[...].reshape(rows, slots * rank) * (1.0 / reps)
    stores = []

    def send(source, target, slot, which):
        store = pltpu.make_async_copy(source.at[slot], target.at[slot], out_sems.at[slot, which])
        store.start()
        stores.append(store)

    for slot in range(slots):
        grad = product(
            averaged[:, slot * rank:(slot + 1) * rank], high_ref[slot], low_ref[slot]
        )
        momentum = momentum_decay * momentum_ref[slot] + grad
        m_ref[slot] = momentum
        send(m_ref, new_momentum_ref, slot, 0)
        change = outer_rate * (grad + momentum_decay * momentum)
        if slot == 0:
            w_ref[0] = first_ref[...] - change
            send(w_ref, new_weights_ref, 0, 1)
        else:
            change_ref[slot] = change
    loads[-1].wait()
    half = lax.broadcasted_iota(jnp.int32, (tile, columns), 0) // (tile // 2)
    for near_core in range(2):

        @pl.when(core == near_core)
        def _():
            for block in range(blocks):
                owner, slot = codes_smem[4 * block], codes_smem[4 * block + 1]
                two, place = codes_smem[4 * block + 2] == 1, codes_smem[4 * block + 3]
                for side, whole, other in (
                    (near_core, near_ref, near_across_ref),
                    (1 - near_core, far_ref, far_across_ref),
                ):
                    here = slice(side * columns, (side + 1) * columns)

                    @pl.when(jnp.logical_not(two))
                    def _():
                        rows_ref[block, :, here] = whole[owner]

                    @pl.when(two)
                    def _():
                        mine, theirs = whole[owner], other[place]
                        keep = slot == across
                        mine = jnp.where(keep, mine, pltpu.roll(mine, tile // 2, 0))
                        theirs = jnp.where(keep, pltpu.roll(theirs, tile // 2, 0), theirs)
                        rows_ref[block, :, here] = jnp.where(half == across, mine, theirs)

    store = pltpu.make_async_copy(rows_ref, replica_ref, rows_sem)
    store.start()
    stores.append(store)
    for slot in range(1, slots):
        loads[slot - 1].wait()
        used = codes_smem[4 * blocks + slot]
        w_ref[slot] = jnp.where(used == 1, w_ref[slot] - change_ref[slot], 0.0)
        send(w_ref, new_weights_ref, slot, 1)
    for store in stores:
        store.wait()


def local(replica_delta, layer_basis, layer_of, owner_of, weights_owned, momentum_owned):
    own_count = lax.axis_size("own")
    rep_count = lax.axis_size("rep")
    slots, owned_rows, width = weights_owned.shape
    blocks, rows = replica_delta.shape[1:3]
    layers, _, rank = layer_basis.shape
    f32, bf16 = jnp.float32, jnp.bfloat16
    shape = jax.ShapeDtypeStruct
    columns = width // 2
    total = columns + slots * rank
    basis = jnp.swapaxes(layer_basis, 1, 2)

    def stay(array):
        return pltpu.with_memory_space_constraint(array, pltpu.HBM)

    weights, momentum = stay(weights_owned), stay(momentum_owned)

    def swap(array, bits):
        pairs = [(rep, rep ^ bits) for rep in range(rep_count)]
        return lax.ppermute(array, "rep", pairs)

    sent, coeffs = pl.pallas_call(
        outset_kernel,
        out_shape=[
            shape((own_count, rows, total), f32),
            shape((own_count, rows, slots * rank), f32),
        ],
        in_specs=[HBM] * 6,
        out_specs=[HBM, VMEM],
        scratch_shapes=[
            pltpu.SMEM(owner_of.shape, jnp.int32),
            pltpu.SMEM(layer_of.shape, jnp.int32),
            pltpu.VMEM(replica_delta.shape[1:], f32),
            pltpu.VMEM(basis.shape, f32),
            pltpu.VMEM((slots, owned_rows, columns), f32),
            pltpu.VMEM((slots, owned_rows, columns), f32),
            pltpu.VMEM((own_count, rows, total), f32),
            pltpu.SemaphoreType.DMA((5 + layers,)),
            pltpu.SemaphoreType.DMA((2,)),
        ],
        compiler_params=params(replica_delta, basis, basis, weights_owned),
        name="outset",
    )(stay(owner_of), stay(layer_of), stay(replica_delta[0]), stay(basis), weights, momentum)
    near = lax.all_to_all(sent, "own", split_axis=0, concat_axis=0, tiled=True)

    coeffs = coeffs + swap(coeffs, 1)
    coeffs = coeffs + swap(coeffs, 2)
    most = blocks // 2
    grad, high, low, held, first, marks, codes = pl.pallas_call(
        lambda *refs: prepare_kernel(rep_count, *refs),
        out_shape=[
            shape((own_count, rows, columns), f32),
            shape((slots, rank, width), bf16),
            shape((slots, rank, width), bf16),
            shape(momentum_owned.shape, f32),
            shape(weights_owned.shape[1:], f32),
            shape((most * own_count, 128), f32),
            shape((4 * blocks + slots,), jnp.int32),
        ],
        in_specs=[SMEM, SMEM, VMEM, HBM, HBM, HBM],
        out_specs=[VMEM] * 6 + [SMEM],
        scratch_shapes=[
            pltpu.VMEM((own_count, rows, layers * rank), f32),
            pltpu.VMEM((layers, rank, columns), f32),
            pltpu.VMEM((slots, rank, width), f32),
            pltpu.SemaphoreType.DMA((3 + slots,)),
        ],
        compiler_params=params(basis, replica_delta, replica_delta, momentum_owned, momentum_owned),
        name="prepare",
    )(owner_of, layer_of, coeffs, stay(basis), momentum, weights)

    def after(array, done):
        return pl.pallas_call(
            after_kernel,
            out_shape=shape(array.shape, f32),
            in_specs=[ANY, ANY],
            out_specs=ANY,
            input_output_aliases={0: 0},
            compiler_params=params(),
            name="after",
        )(array, done)

    near = after(near, grad)
    new, given = pl.pallas_call(
        select_kernel,
        out_shape=[
            shape((own_count, rows, columns), f32),
            shape((most, rows, columns), f32),
        ],
        in_specs=[VMEM] * 3,
        out_specs=[VMEM] * 2,
        compiler_params=params(near, near, near, marks),
        name="select",
    )(near, grad, marks)

    def finish(count, codes, near, new, given, high, low, held, first, weights_owned):
        partial = near[:, :, columns:]
        partial = (partial + swap(partial, 1)) + (swap(partial, 2) + swap(partial, 3))
        far = swap(new, 1)
        near_across = swap(given[:count], 2)
        far_across = swap(near_across, 1)
        return pl.pallas_call(
            lambda *refs: final_kernel(rep_count, *refs),
            out_shape=[
                shape(weights_owned.shape, f32),
                shape(weights_owned.shape, f32),
                shape((blocks, rows, width), f32),
            ],
            in_specs=[HBM] + [VMEM] * 9 + [HBM],
            out_specs=[HBM] * 3,
            scratch_shapes=[
                pltpu.SMEM(codes.shape, jnp.int32),
                pltpu.VMEM(weights_owned.shape, f32),
                pltpu.VMEM(weights_owned.shape, f32),
                pltpu.VMEM(weights_owned.shape, f32),
                pltpu.VMEM((blocks, rows, width), f32),
                pltpu.SemaphoreType.DMA((slots,)),
                pltpu.SemaphoreType.DMA((slots, 2)),
                pltpu.SemaphoreType.DMA(()),
            ],
            compiler_params=params(basis, *[weights_owned] * 3, replica_delta, replica_delta),
            name="final",
        )(
            stay(codes), partial, high, low, held, first,
            new, near_across, far, far_across, stay(weights_owned),
        )

    pairs = jnp.sum(owner_of[:, None] == owner_of[None, :], dtype=jnp.int32) - blocks
    unit = max(1, most // 4)
    counts = [min(most, unit * (index + 1)) for index in range(-(-most // unit))]
    return tuple(lax.switch(
        (pairs // 2 + unit - 1) // unit - 1,
        [functools.partial(finish, count) for count in counts],
        codes, near, new, given, high, low, held, first, weights_owned,
    ))


def solution(mesh):
    placed = (
        P("rep", None, "own", None),
        P(),
        P(),
        P(),
        P("own", None, None),
        P("own", None, None),
    )
    return jax.shard_map(
        local,
        mesh=mesh,
        in_specs=placed,
        out_specs=(P("own", None, None), P("own", None, None), P(None, "own", None)),
        check_vma=False,
    )
```

```python
import functools
import math

import jax
import jax.numpy as jnp
from jax import lax
from jax.experimental import pallas as pl
from jax.experimental.pallas import tpu as pltpu
from jax.sharding import PartitionSpec as P

momentum_decay = 0.9
outer_rate = 0.7
carried = outer_rate * momentum_decay * momentum_decay
total_rate = outer_rate * (1.0 + momentum_decay)

VMEM = pl.BlockSpec(memory_space=pltpu.VMEM)
SMEM = pl.BlockSpec(memory_space=pltpu.SMEM)
HBM = pl.BlockSpec(memory_space=pltpu.HBM)
ANY = pl.BlockSpec(memory_space=pl.ANY)


def params(*arrays):
    held = sum(4 * math.prod(array.shape) for array in arrays)
    return pltpu.CompilerParams(vmem_limit_bytes=2 * held + 4 * 1024 * 1024)


def position():
    rep = lax.axis_index("rep")
    return lax.rem(rep, 2), rep // 2


def split(array):
    high = array.astype(jnp.bfloat16)
    low = (array - high.astype(jnp.float32)).astype(jnp.bfloat16)
    return high, low


def product(left, right_high, right_low, contract=((1,), (0,))):
    rows = left.shape[0]
    high, low = split(left)

    def dot(a, b):
        return lax.dot_general(
            a, b, (contract, ((), ())), preferred_element_type=jnp.float32
        )

    both = dot(jnp.concatenate([high, low], axis=0), right_high)
    return both[:rows] + (both[rows:] + dot(high, right_low))


def place_of(owner_ref, block):
    owner = owner_ref[block]
    slot = jnp.int32(0)
    for earlier in range(block):
        slot = slot + jnp.where(owner_ref[earlier] == owner, 1, 0)
    return owner, slot


def shared(places, block):
    owner, _ = places[block]
    held, before = jnp.int32(0), jnp.int32(0)
    for other_owner, other_slot in places:
        held = held + jnp.where(other_owner == owner, 1, 0)
        before = before + jnp.where((other_slot == 1) & (other_owner < owner), 1, 0)
    return held == 2, before


def outset_kernel(
    owner_ref, layer_ref, delta_ref, basis_ref, weights_ref, momentum_ref,
    sent_ref, coeffs_ref,
    owner_smem, layer_smem, delta_vmem, basis_vmem, w_ref, m_ref, made_ref, in_sems, out_sems,
):
    owners, rows, total = sent_ref.shape
    blocks, _, width = delta_ref.shape
    layers, rank, _ = basis_ref.shape
    columns = width // 2
    core, across = position()
    part = pl.ds(pl.multiple_of(core * columns, 128), columns)
    loads = [
        pltpu.make_async_copy(source, target, in_sems.at[index])
        for index, (source, target) in enumerate((
            (delta_ref, delta_vmem),
            *[(basis_ref.at[layer], basis_vmem.at[layer]) for layer in range(layers)],
            (weights_ref.at[:, :, part], w_ref),
            (momentum_ref.at[:, :, part], m_ref),
            (owner_ref, owner_smem),
            (layer_ref, layer_smem),
        ))
    ]
    for load in loads:
        load.start()
    for load in loads[:1 + layers]:
        load.wait()
    high, low = split(basis_vmem[...].reshape(layers * rank, width))
    products = product(delta_vmem[...].reshape(blocks * rows, width), high, low, ((1,), (1,)))
    for load in loads[1 + layers:]:
        load.wait()
    upper = lax.broadcasted_iota(jnp.int32, (rows, columns), 0) < rows // 2
    me = lax.axis_index("own")
    held = jnp.int32(0)
    for block in range(blocks):
        held = held + jnp.where(owner_smem[block] == me, 1, 0)
    for owner in range(owners):
        here = pl.ds(owner * rows, rows)
        first, second = [
            w_ref[slot, here, :] - carried * m_ref[slot, here, :] for slot in range(2)
        ]
        halves = jnp.where(
            across == 0,
            jnp.where(upper, first, pltpu.roll(second, rows // 2, 0)),
            jnp.where(upper, pltpu.roll(first, rows // 2, 0), second),
        )
        made_ref[owner, :, :columns] = jnp.where(held == 2, halves, first)
    early = pltpu.make_async_copy(
        made_ref.at[:, :, :columns], sent_ref.at[:, :, :columns], out_sems.at[0]
    )
    early.start()
    lane = lax.broadcasted_iota(jnp.int32, (rows, 2 * rank), 1)
    coeffs_ref[...] = jnp.zeros_like(coeffs_ref)
    for block in range(blocks):
        owner, slot = place_of(owner_smem, block)
        folded = jnp.zeros((rows, 2 * rank), jnp.float32)
        for pair in range(layers // 2):
            own = products[block * rows:(block + 1) * rows, 2 * rank * pair:2 * rank * (pair + 1)]
            folded = folded + jnp.where(2 * pair + lane // rank == layer_smem[block], own, 0.0)
        folded = folded + pltpu.roll(folded, rank, 1)
        pltpu.store(coeffs_ref.at[owner], folded, mask=lane // rank == slot)
    made_ref[:, :, columns:] = coeffs_ref[...]
    late = pltpu.make_async_copy(
        made_ref.at[:, :, columns:], sent_ref.at[:, :, columns:], out_sems.at[1]
    )
    late.start()
    early.wait()
    late.wait()


def held_by(me, slot, owner_ref, layer_ref):
    used, layer = jnp.int32(0), jnp.int32(0)
    for block in range(owner_ref.shape[0]):
        owner, place = place_of(owner_ref, block)
        here = (owner == me) & (place == slot)
        layer = jnp.where(here, layer_ref[block], layer)
        used = jnp.where(here, 1, used)
    return used, layer


def prepare_kernel(
    reps, owner_ref, layer_ref, coeffs_ref, basis_ref, momentum_ref, weights_ref,
    grad_ref, high_ref, low_ref, held_ref, first_ref, marks_ref, codes_ref,
    wide_ref, basis_vmem, slot_vmem, sems,
):
    owners, rows, columns = grad_ref.shape
    blocks = owner_ref.shape[0]
    layers, rank, width = basis_ref.shape
    slots = momentum_ref.shape[0]
    me = lax.axis_index("own")
    core, across = position()
    part = pl.ds(pl.multiple_of(core * columns, 128), columns)
    found = [held_by(me, slot, owner_ref, layer_ref) for slot in range(slots)]
    loads = [pltpu.make_async_copy(basis_ref.at[:, :, part], basis_vmem, sems.at[0])]
    for slot in range(slots):
        loads.append(
            pltpu.make_async_copy(basis_ref.at[found[slot][1]], slot_vmem.at[slot], sems.at[1 + slot])
        )
    loads.append(pltpu.make_async_copy(momentum_ref, held_ref, sems.at[1 + slots]))
    loads.append(pltpu.make_async_copy(weights_ref.at[0], first_ref, sems.at[2 + slots]))
    for load in loads:
        load.start()
    lane = lax.broadcasted_iota(jnp.int32, (rows, 2 * rank), 1)
    wide_lane = lax.broadcasted_iota(jnp.int32, (rows, layers * rank), 1)
    half = lax.broadcasted_iota(jnp.int32, (rows, layers * rank), 0) // (rows // 2)
    wide_ref[...] = jnp.zeros_like(wide_ref)
    marks_ref[...] = jnp.zeros_like(marks_ref)
    places = [place_of(owner_ref, block) for block in range(blocks)]
    for block in range(blocks):
        owner, slot = places[block]
        two, before = shared(places, block)
        both = jnp.where(lane // rank == slot, coeffs_ref[owner], 0.0)
        both = both + pltpu.roll(both, rank, 1)
        wide = jnp.concatenate([both] * (layers // 2), axis=1)
        wide = jnp.where(wide_lane // rank == layer_ref[block], wide, 0.0)
        codes_ref[4 * block] = owner
        codes_ref[4 * block + 1] = slot
        codes_ref[4 * block + 2] = jnp.where(two, 1, 0)
        codes_ref[4 * block + 3] = jnp.where(two, before, 0)
        halves = jnp.where(slot == across, wide, pltpu.roll(wide, rows // 2, 0))
        halves = jnp.where(half == slot, halves, 0.0)
        wide_ref[owner] = wide_ref[owner] + jnp.where(two, halves, wide)

        @pl.when(slot == 1)
        def _():
            marks_ref[pl.ds(before * owners + owner, 1), :] = jnp.ones(
                (1, marks_ref.shape[1]), jnp.float32
            )

    loads[0].wait()
    high, low = split(basis_vmem[...].reshape(layers * rank, columns))
    wide = wide_ref[...].reshape(owners * rows, layers * rank)
    grad = product(wide * (total_rate / reps), high, low)
    grad_ref[...] = grad.reshape(owners, rows, columns)
    for slot in range(slots):
        loads[1 + slot].wait()
        slot_high, slot_low = split(slot_vmem[slot])
        high_ref[slot] = slot_high
        low_ref[slot] = slot_low
    loads[-2].wait()
    loads[-1].wait()
    for slot in range(slots):
        codes_ref[4 * blocks + slot] = found[slot][0]

        @pl.when(found[slot][0] == 0)
        def _():
            high_ref[slot] = jnp.zeros_like(high_ref[slot])
            low_ref[slot] = jnp.zeros_like(low_ref[slot])
            held_ref[slot] = jnp.zeros_like(held_ref[slot])
            if slot == 0:
                first_ref[...] = jnp.zeros_like(first_ref)


def select_kernel(near_ref, grad_ref, marks_ref, new_ref, given_ref):
    _, rows, columns = given_ref.shape
    owners = near_ref.shape[0]
    lanes = marks_ref.shape[1]
    for owner in range(owners):
        new_ref[owner, :, :columns] = near_ref[owner, :, :columns] - grad_ref[owner]
    new_ref[:, :, columns:] = near_ref[:, :, columns:]

    def one(place, carry):
        total = jnp.zeros((rows, columns), jnp.float32)
        for owner in range(owners):
            mark = marks_ref[pl.ds(place * owners + owner, 1), :]
            mark = jnp.concatenate([mark] * (columns // lanes), axis=1)
            total = total + mark * new_ref[owner, :, :columns]
        given_ref[place] = total
        return carry

    lax.fori_loop(0, given_ref.shape[0], one, 0, unroll=given_ref.shape[0] <= 4)


def after_kernel(rows_ref, done_ref, same_ref):
    pass


def final_kernel(
    reps, codes_ref, coeffs_ref, high_ref, low_ref, momentum_ref, first_ref,
    near_ref, near_across_ref, far_ref, far_across_ref, weights_ref,
    new_weights_ref, new_momentum_ref, replica_ref,
    codes_smem, w_ref, m_ref, change_ref, rows_ref, in_sems, out_sems, rows_sem,
):
    slots, rows, width = weights_ref.shape
    rank = high_ref.shape[1]
    blocks = replica_ref.shape[0]
    _, tile, columns = near_across_ref.shape
    core, across = position()
    sources = [(weights_ref.at[slot], w_ref.at[slot]) for slot in range(1, slots)]
    sources.append((codes_ref, codes_smem))
    loads = [
        pltpu.make_async_copy(source, target, in_sems.at[index])
        for index, (source, target) in enumerate(sources)
    ]
    for load in loads:
        load.start()
    averaged = coeffs_ref[...].reshape(rows, slots * rank) * (1.0 / reps)
    stores = []

    def send(source, target, slot, which):
        store = pltpu.make_async_copy(source.at[slot], target.at[slot], out_sems.at[slot, which])
        store.start()
        stores.append(store)

    for slot in range(slots):
        grad = product(
            averaged[:, slot * rank:(slot + 1) * rank], high_ref[slot], low_ref[slot]
        )
        momentum = momentum_decay * momentum_ref[slot] + grad
        m_ref[slot] = momentum
        send(m_ref, new_momentum_ref, slot, 0)
        change = outer_rate * (grad + momentum_decay * momentum)
        if slot == 0:
            w_ref[0] = first_ref[...] - change
            send(w_ref, new_weights_ref, 0, 1)
        else:
            change_ref[slot] = change
    loads[-1].wait()
    half = lax.broadcasted_iota(jnp.int32, (tile, columns), 0) // (tile // 2)
    for near_core in range(2):

        @pl.when(core == near_core)
        def _():
            for block in range(blocks):
                owner, slot = codes_smem[4 * block], codes_smem[4 * block + 1]
                two, place = codes_smem[4 * block + 2] == 1, codes_smem[4 * block + 3]
                for side, whole, other in (
                    (near_core, near_ref, near_across_ref),
                    (1 - near_core, far_ref, far_across_ref),
                ):
                    here = slice(side * columns, (side + 1) * columns)

                    @pl.when(jnp.logical_not(two))
                    def _():
                        rows_ref[block, :, here] = whole[owner, :, :columns]

                    @pl.when(two)
                    def _():
                        mine, theirs = whole[owner, :, :columns], other[place]
                        keep = slot == across
                        mine = jnp.where(keep, mine, pltpu.roll(mine, tile // 2, 0))
                        theirs = jnp.where(keep, pltpu.roll(theirs, tile // 2, 0), theirs)
                        rows_ref[block, :, here] = jnp.where(half == across, mine, theirs)

    store = pltpu.make_async_copy(rows_ref, replica_ref, rows_sem)
    store.start()
    stores.append(store)
    for slot in range(1, slots):
        loads[slot - 1].wait()
        used = codes_smem[4 * blocks + slot]
        w_ref[slot] = jnp.where(used == 1, w_ref[slot] - change_ref[slot], 0.0)
        send(w_ref, new_weights_ref, slot, 1)
    for store in stores:
        store.wait()


def local(replica_delta, layer_basis, layer_of, owner_of, weights_owned, momentum_owned):
    own_count = lax.axis_size("own")
    rep_count = lax.axis_size("rep")
    slots, owned_rows, width = weights_owned.shape
    blocks, rows = replica_delta.shape[1:3]
    layers, _, rank = layer_basis.shape
    f32, bf16 = jnp.float32, jnp.bfloat16
    shape = jax.ShapeDtypeStruct
    columns = width // 2
    total = columns + slots * rank
    basis = jnp.swapaxes(layer_basis, 1, 2)

    def stay(array):
        return pltpu.with_memory_space_constraint(array, pltpu.HBM)

    weights, momentum = stay(weights_owned), stay(momentum_owned)

    def swap(array, bits):
        pairs = [(rep, rep ^ bits) for rep in range(rep_count)]
        return lax.ppermute(array, "rep", pairs)

    sent, coeffs = pl.pallas_call(
        outset_kernel,
        out_shape=[
            shape((own_count, rows, total), f32),
            shape((own_count, rows, slots * rank), f32),
        ],
        in_specs=[HBM] * 6,
        out_specs=[HBM, VMEM],
        scratch_shapes=[
            pltpu.SMEM(owner_of.shape, jnp.int32),
            pltpu.SMEM(layer_of.shape, jnp.int32),
            pltpu.VMEM(replica_delta.shape[1:], f32),
            pltpu.VMEM(basis.shape, f32),
            pltpu.VMEM((slots, owned_rows, columns), f32),
            pltpu.VMEM((slots, owned_rows, columns), f32),
            pltpu.VMEM((own_count, rows, total), f32),
            pltpu.SemaphoreType.DMA((5 + layers,)),
            pltpu.SemaphoreType.DMA((2,)),
        ],
        compiler_params=params(replica_delta, basis, basis, weights_owned),
        name="outset",
    )(stay(owner_of), stay(layer_of), stay(replica_delta[0]), stay(basis), weights, momentum)
    near = lax.all_to_all(sent, "own", split_axis=0, concat_axis=0, tiled=True)

    coeffs = coeffs + swap(coeffs, 1)
    coeffs = coeffs + swap(coeffs, 2)
    most = blocks // 2
    grad, high, low, held, first, marks, codes = pl.pallas_call(
        lambda *refs: prepare_kernel(rep_count, *refs),
        out_shape=[
            shape((own_count, rows, columns), f32),
            shape((slots, rank, width), bf16),
            shape((slots, rank, width), bf16),
            shape(momentum_owned.shape, f32),
            shape(weights_owned.shape[1:], f32),
            shape((most * own_count, 128), f32),
            shape((4 * blocks + slots,), jnp.int32),
        ],
        in_specs=[SMEM, SMEM, VMEM, HBM, HBM, HBM],
        out_specs=[VMEM] * 6 + [SMEM],
        scratch_shapes=[
            pltpu.VMEM((own_count, rows, layers * rank), f32),
            pltpu.VMEM((layers, rank, columns), f32),
            pltpu.VMEM((slots, rank, width), f32),
            pltpu.SemaphoreType.DMA((3 + slots,)),
        ],
        compiler_params=params(basis, replica_delta, replica_delta, momentum_owned, momentum_owned),
        name="prepare",
    )(owner_of, layer_of, coeffs, stay(basis), momentum, weights)

    def after(array, done):
        return pl.pallas_call(
            after_kernel,
            out_shape=shape(array.shape, f32),
            in_specs=[ANY, ANY],
            out_specs=ANY,
            input_output_aliases={0: 0},
            compiler_params=params(),
            name="after",
        )(array, done)

    near = after(near, grad)
    new, given = pl.pallas_call(
        select_kernel,
        out_shape=[
            shape(near.shape, f32),
            shape((most, rows, columns), f32),
        ],
        in_specs=[VMEM] * 3,
        out_specs=[VMEM] * 2,
        compiler_params=params(near, near, near, marks),
        name="select",
    )(near, grad, marks)

    def finish(count, codes, new, given, high, low, held, first, weights_owned):
        partial = new[:, :, columns:]
        far = swap(new, 1)
        partial = (partial + far[:, :, columns:]) + (swap(partial, 2) + swap(partial, 3))
        near_across = swap(given[:count], 2)
        far_across = swap(near_across, 1)
        return pl.pallas_call(
            lambda *refs: final_kernel(rep_count, *refs),
            out_shape=[
                shape(weights_owned.shape, f32),
                shape(weights_owned.shape, f32),
                shape((blocks, rows, width), f32),
            ],
            in_specs=[HBM] + [VMEM] * 9 + [HBM],
            out_specs=[HBM] * 3,
            scratch_shapes=[
                pltpu.SMEM(codes.shape, jnp.int32),
                pltpu.VMEM(weights_owned.shape, f32),
                pltpu.VMEM(weights_owned.shape, f32),
                pltpu.VMEM(weights_owned.shape, f32),
                pltpu.VMEM((blocks, rows, width), f32),
                pltpu.SemaphoreType.DMA((slots,)),
                pltpu.SemaphoreType.DMA((slots, 2)),
                pltpu.SemaphoreType.DMA(()),
            ],
            compiler_params=params(basis, *[weights_owned] * 3, replica_delta, replica_delta),
            name="final",
        )(
            stay(codes), partial, high, low, held, first,
            new, near_across, far, far_across, stay(weights_owned),
        )

    pairs = jnp.sum(owner_of[:, None] == owner_of[None, :], dtype=jnp.int32) - blocks
    unit = max(1, most // 4)
    counts = [min(most, unit * (index + 1)) for index in range(-(-most // unit))]
    return tuple(lax.switch(
        (pairs // 2 + unit - 1) // unit - 1,
        [functools.partial(finish, count) for count in counts],
        codes, new, given, high, low, held, first, weights_owned,
    ))


def solution(mesh):
    placed = (
        P("rep", None, "own", None),
        P(),
        P(),
        P(),
        P("own", None, None),
        P("own", None, None),
    )
    return jax.shard_map(
        local,
        mesh=mesh,
        in_specs=placed,
        out_specs=(P("own", None, None), P("own", None, None), P(None, "own", None)),
        check_vma=False,
    )
```
